256 devices in a mesh: dx: 16 (over z_lo, x, core), dy: 4 (over z_hi), band: 4 (over y).
Axes of the slice: x: 4, y: 4, z: 8 (z_hi: 4, z_lo: 2; z = z_hi * 2 + z_lo), core: 2. Of those that a mesh axis runs over, the one named last changes fastest.
Arguments:
- band_fields: float32 [8, 80, 320, 320], P('band', 'dx', 'dy'), may hold values from -36 to 36
- potential: float32 [80, 320, 320], P('dx', 'dy'), may hold values from -2 to 1
- cutoff: float32 [1], replicated, may hold values from 1 to 2
- upper_bound: float32 [1], replicated, may hold values from 11 to 12.5
Outputs:
- rotated: float32 [8, 80, 320, 320], P('band', 'dx', 'dy')
The draws below stay inside these ranges and needn't reach their ends.
All inputs are finite; a program needn't handle non-finite values.
Results may differ from the reference program's by a relative error of at most 0.000075.
Values sent between devices are 32-bit elements; how exact they have to be, the bound alone decides.
No kernel may reach another device: no remote copies, remote signals or barrier semaphores. Data moves between devices by JAX's collectives and lax.ppermute only.
A program may use at most 64 MiB of HBM per device.

```python
import math
import jax
import jax.numpy as jnp
from jax import lax

NZ = 320
DEGREE = 4
NBANDS = 8
NX = 80
NY = 320


def draw_band_fields(key, part):
    key = jax.random.fold_in(key, 7)
    key_noise, key_common, key_mixing, key_scale = jax.random.split(key, 4)
    random_part = jax.random.truncated_normal(key_noise, -4.0, 4.0, (NBANDS, NX, NY, NZ), jnp.float32)
    common = jax.random.truncated_normal(key_common, -4.0, 4.0, (1, NX, NY, NZ), jnp.float32)
    rise_log = math.log(3.0)
    mixing = jax.random.uniform(key_mixing, (NBANDS, 1, 1, 1), jnp.float32, -1.0, 1.0)
    across = jnp.arange(NX, dtype=jnp.float32).reshape(1, NX, 1, 1) / NX
    column = jax.random.uniform(key_scale, (1, NX, NY, 1), jnp.float32, 0.0, math.log(4.0))
    envelope = 0.3 * jnp.exp(rise_log * across + column)
    return envelope * (random_part + 0.8 * mixing * common)


def block_scale(stream_key, shape, cuts, low, top_value):
    factor_of = 1.0
    for axis_at, parts in cuts:
        heights = jax.random.uniform(jax.random.fold_in(jax.random.fold_in(stream_key, 6), axis_at), (parts,), jnp.float32, low / len(cuts), top_value / len(cuts))
        factor_of = factor_of * jnp.repeat(jnp.exp(heights), shape[axis_at] // parts).reshape((-1,) + (1,) * (len(shape) - 1 - axis_at))
    return factor_of


def setup_inputs(seed: int = 0) -> dict:
    splits = jax.random.split(jax.random.key(seed), 5)
    band_fields = draw_band_fields(jax.random.fold_in(splits[4], 71), 0)
    potential = jnp.clip(-2.0 + 3.0 * jax.random.uniform(splits[1], (NX, NY, NZ), jnp.float32) ** block_scale(splits[1], (NX, NY, NZ), ((0, 16), (1, 4)), -0.2, 0.2), -2.0, 1.0)
    cutoff = jnp.clip(jax.random.uniform(splits[2], (1,), jnp.float32, 1.0, 2.0), 1.0, 2.0)
    upper_bound = jnp.clip(jax.random.uniform(splits[3], (1,), jnp.float32, 11.0, 12.5), 11.0, 12.5)
    return {"band_fields": band_fields, "potential": potential, "cutoff": cutoff, "upper_bound": upper_bound}


stencil_weights = (-205.0 / 72.0, 8.0 / 5.0, -1.0 / 5.0, 8.0 / 315.0, -1.0 / 560.0)

def lower_inverse(factor):
    extent = factor.shape[0]
    identity = jnp.eye(extent, dtype=factor.dtype)
    inverse_rows = []
    for target in range(extent):
        running = identity[target]
        for source in range(target):
            running = running - factor[target, source] * inverse_rows[source]
        inverse_rows.append(running / factor[target, target])
    return jnp.stack(inverse_rows)

def shifted_apply(source_field, potential, center, half_width):
    laplace = 3.0 * stencil_weights[0] * source_field
    for offset in range(1, 5):
        for axis_index in (0, 1, 2):
            laplace = laplace + stencil_weights[offset] * (jnp.roll(source_field, offset, axis_index) + jnp.roll(source_field, -offset, axis_index))
    energy = -0.5 * laplace + potential * source_field
    return (energy - center * source_field) / half_width

def reference(band_fields, potential, cutoff, upper_bound):
    center = 0.5 * (cutoff[0] + upper_bound[0])
    half_width = 0.5 * (upper_bound[0] - cutoff[0])

    def filter_band(source_field):
        previous = source_field
        current = shifted_apply(source_field, potential, center, half_width)
        for degree in range(DEGREE - 1):
            following = 2.0 * shifted_apply(current, potential, center, half_width) - previous
            previous = current
            current = following
        return current
    filtered = lax.map(filter_band, band_fields)
    flattened = filtered.reshape(filtered.shape[0], -1)
    correlation = jnp.dot(flattened, flattened.T, precision=lax.Precision.HIGHEST) / float(NX * NY * NZ)
    inverse = lower_inverse(jnp.linalg.cholesky(correlation))
    rotated = jnp.dot(inverse, flattened, precision=lax.Precision.HIGHEST)
    return rotated.reshape(filtered.shape)
```

```python
import functools

import jax
import jax.numpy as jnp
from jax import lax
from jax.experimental import pallas as pl
from jax.experimental.pallas import tpu as pltpu
from jax.sharding import PartitionSpec as P

BANDS = 2
LAYERS = 5
WIDTH = 4
GROUPS = 4
F32 = jnp.float32

stencil_weights = (-205.0 / 72.0, 8.0 / 5.0, -1.0 / 5.0, 8.0 / 315.0, -1.0 / 560.0)

STATE = (BANDS, LAYERS, 3, 10, 8, 128)
SIDE = (BANDS, WIDTH, 25, 8, 128)
EDGE = (BANDS, 64, 128)
PIECE = (BANDS, 32, 8, 128)


def call(kernel, outs, scratch=(), in_specs=None, cost=4_000_000):
    kwargs = {} if in_specs is None else {"in_specs": in_specs}
    return pl.pallas_call(
        kernel,
        out_shape=tuple(jax.ShapeDtypeStruct(shape, F32) for shape in outs),
        scratch_shapes=[pltpu.VMEM(shape, F32) for shape in scratch],
        compiler_params=pltpu.CompilerParams(vmem_limit_bytes=40 * 1024 * 1024),
        cost_estimate=pl.CostEstimate(flops=cost, bytes_accessed=4_000_000, transcendentals=0),
        **kwargs,
    )


def lanes():
    return lax.broadcasted_iota(jnp.int32, (8, 128), 1)


def sublanes():
    return lax.broadcasted_iota(jnp.int32, (8, 128), 0)


def pair(low, high):
    return jnp.where(lanes() < 64, low, pltpu.roll(high, 64, 1))


def bounds(cutoff_ref, upper_ref):
    low = jnp.full((8, 128), cutoff_ref[0], F32)
    high = jnp.full((8, 128), upper_ref[0], F32)
    return 0.5 * (low + high), 1.0 / (0.5 * (high - low))


def send_sides(tiles, band, layer, low_ref, high_ref):
    for tile in range(2):
        for j in range(10):
            if layer < WIDTH:
                low_ref[band, layer, tile * 10 + j] = tiles[tile][j]
            if layer >= 1:
                high_ref[band, layer - 1, tile * 10 + j] = tiles[tile][j]
    for j in range(5):
        both = pair(tiles[2][j], tiles[2][j + 5])
        if layer < WIDTH:
            low_ref[band, layer, 20 + j] = both
        if layer >= 1:
            high_ref[band, layer - 1, 20 + j] = both


def send_edges(tiles, band, layer, low_ref, high_ref):
    for tile in range(3):
        for j in range(4):
            row = j * 16 + layer * 3 + tile
            low_ref[band, row : row + 1, :] = tiles[tile][j][0:1]
            high_ref[band, row : row + 1, :] = tiles[tile][6 + j][7:8]


def clear_edges(band, *refs):
    for ref in refs:
        for j in range(4):
            ref[band, j * 16 + 15 : j * 16 + 16, :] = jnp.zeros((1, 128), F32)


def split_kernel(field_ref, state_ref, side_low_ref, side_high_ref, edge_low_ref, edge_high_ref, stage_ref):
    def one_band(band, carry):
        for layer in range(LAYERS):
            for tile in range(2):
                stage_ref[tile] = field_ref[band, layer, :, tile * 128 : tile * 128 + 128]
            stage_ref[2, :, 0:64] = field_ref[band, layer, :, 256:320]
            tiles = [[stage_ref[tile, pl.ds(j, 8, stride=10), :] for j in range(10)] for tile in range(3)]
            for tile in range(3):
                for j in range(10):
                    state_ref[band, layer, tile, j] = tiles[tile][j]
            send_sides(tiles, band, layer, side_low_ref, side_high_ref)
            send_edges(tiles, band, layer, edge_low_ref, edge_high_ref)
        clear_edges(band, edge_low_ref, edge_high_ref)
        return carry

    lax.fori_loop(0, BANDS, one_band, 0)


def inner_kernel(first, *refs):
    if first:
        state_ref, potential_ref, cutoff_ref, upper_ref, out_ref, diagonal_ref, wide_ref, stage_ref = refs
    else:
        state_ref, previous_ref, diagonal_ref, cutoff_ref, upper_ref, out_ref, wide_ref = refs
    center, per_half_width = bounds(cutoff_ref, upper_ref)
    if first:
        shift = center + 1.5 * stencil_weights[0]
        for layer in range(LAYERS):
            for tile in range(2):
                stage_ref[tile] = potential_ref[layer, :, tile * 128 : tile * 128 + 128]
            stage_ref[2, :, 0:64] = potential_ref[layer, :, 256:320]
            for tile in range(3):
                for j in range(10):
                    diagonal_ref[layer, tile, j] = (stage_ref[tile, pl.ds(j, 8, stride=10), :] - shift) * per_half_width
    factor = 1.0 if first else 2.0
    weights = [None] + [(-0.5 * factor * stencil_weights[k]) * per_half_width for k in range(1, 5)]
    lane = lanes()
    row = sublanes()

    def one_band(band, carry):
        def widen(j, carry):
            for layer in range(LAYERS):
                tiles = [state_ref[band, layer, tile, j] for tile in range(3)]
                tiles[2] = jnp.where(
                    lane < 64,
                    tiles[2],
                    jnp.where(lane < 96, pltpu.roll(tiles[0], 64, 1), pltpu.roll(tiles[2], 64, 1)),
                )
                for tile in range(3):
                    wide_ref[layer, tile, j + 4] = tiles[tile]
            return carry

        lax.fori_loop(0, 10, widen, 0)

        def wrap(j, carry):
            for layer in range(LAYERS):
                for tile in range(3):
                    above = wide_ref[layer, tile, j + 4]
                    wide_ref[layer, tile, j + 14] = jnp.where(row < 7, pltpu.roll(above, 7, 0), 0.0)
                    below = wide_ref[layer, tile, j + 10]
                    wide_ref[layer, tile, j] = jnp.where(row > 0, pltpu.roll(below, 1, 0), 0.0)
            return carry

        lax.fori_loop(0, 4, wrap, 0)

        def rows(j, carry):
            mids = [[wide_ref[layer, tile, j + 4] for tile in range(3)] for layer in range(LAYERS)]
            for layer in range(LAYERS):
                mid = mids[layer]
                totals = [None] * 3
                for k in range(1, 5):
                    ups = [pltpu.roll(mid[tile], 128 - k, 1) for tile in range(3)]
                    downs = [pltpu.roll(mid[tile], k, 1) for tile in range(3)]
                    for tile in range(3):
                        up = ups[2] if tile == 2 else jnp.where(lane < 128 - k, ups[tile], ups[tile + 1])
                        down = jnp.where(lane < k, downs[(tile + 2) % 3], downs[tile])
                        total = up + down
                        total += wide_ref[layer, tile, j + 4 + k] + wide_ref[layer, tile, j + 4 - k]
                        if layer + k < LAYERS:
                            total += mids[layer + k][tile]
                        if layer - k >= 0:
                            total += mids[layer - k][tile]
                        total = weights[k] * total
                        totals[tile] = total if totals[tile] is None else totals[tile] + total
                for tile in range(3):
                    diagonal = diagonal_ref[layer, tile, j] * mid[tile]
                    if first:
                        out_ref[band, layer, tile, j] = totals[tile] + diagonal
                    else:
                        out_ref[band, layer, tile, j] = (
                            totals[tile] + 2.0 * diagonal - previous_ref[band, layer, tile, j]
                        )
            return carry

        return lax.fori_loop(0, 10, rows, carry)

    lax.fori_loop(0, BANDS, one_band, 0)


def outer_kernel(first, last, *refs):
    part_ref, low_ref, high_ref, below_ref, above_ref, cutoff_ref, upper_ref, *refs = refs
    if last:
        group_ref, *piece_refs, whole_ref, rim_ref = refs
    else:
        state_ref, side_low_ref, side_high_ref, edge_low_ref, edge_high_ref, rim_ref = refs
    _, per_half_width = bounds(cutoff_ref, upper_ref)
    factor = 1.0 if first else 2.0
    weights = [None] + [(-0.5 * factor * stencil_weights[k]) * per_half_width for k in range(1, 5)]
    row = sublanes()

    def one_band(band, carry):
        for half in range(2):
            below = [below_ref[band, 16 * j + 8 * half : 16 * j + 8 * half + 8, :] for j in range(4)]
            above = [above_ref[band, 16 * j + 8 * half : 16 * j + 8 * half + 8, :] for j in range(4)]
            for j in range(4):
                rim_ref[0, j, 8 * half : 8 * half + 8, :] = sum(
                    weights[k] * below[4 + j - k] for k in range(j + 1, 5)
                )
                rim_ref[1, j, 8 * half : 8 * half + 8, :] = sum(
                    weights[k] * above[j + 6 + k - 10] for k in range(4 - j, 5)
                )
        for layer in range(LAYERS):
            outside = []
            for v in range(25):
                terms = [weights[layer + 4 - i] * low_ref[band, i, v] for i in range(layer, 4)]
                terms += [weights[5 + i - layer] * high_ref[band, i, v] for i in range(layer)]
                outside.append((terms[0] + terms[1]) + (terms[2] + terms[3]))
            tiles = []
            for tile in range(3):
                cells = []
                for j in range(10):
                    if tile < 2:
                        extra = outside[tile * 10 + j]
                    elif j < 5:
                        extra = outside[20 + j]
                    else:
                        extra = pltpu.roll(outside[15 + j], 64, 1)
                    cell = part_ref[band, layer, tile, j] + extra
                    at = layer * 3 + tile
                    if j < 4:
                        cell += jnp.where(row == 0, rim_ref[0, j, at : at + 1, :], 0.0)
                    if j >= 6:
                        cell += jnp.where(row == 7, rim_ref[1, j - 6, at : at + 1, :], 0.0)
                    cells.append(cell)
                tiles.append(cells)
            if last:
                packed = tiles[0] + tiles[1] + [pair(tiles[2][j], tiles[2][j + 5]) for j in range(5)]
                for v in range(25):
                    place = layer * 25 + v
                    whole_ref[place // 32, band, place % 32] = packed[v]
            else:
                for tile in range(3):
                    for j in range(10):
                        state_ref[band, layer, tile, j] = tiles[tile][j]
                send_sides(tiles, band, layer, side_low_ref, side_high_ref)
                send_edges(tiles, band, layer, edge_low_ref, edge_high_ref)
        if last:
            for place in range(125, 128):
                whole_ref[place // 32, band, place % 32] = jnp.zeros((8, 128), F32)
        else:
            clear_edges(band, edge_low_ref, edge_high_ref)
        return carry

    lax.fori_loop(0, BANDS, one_band, 0)
    if last:
        deal(group_ref[0], whole_ref, piece_refs)


def deal(group, whole_ref, piece_refs):
    for step, piece_ref in enumerate(piece_refs):
        piece_ref[...] = whole_ref[lax.rem(group + step, GROUPS)]


def collect(group, piece_refs, whole_ref):
    for step, piece_ref in enumerate(piece_refs):
        whole_ref[lax.rem(group + GROUPS - step, GROUPS)] = piece_ref[...]


PAIRS = [(a, b) for a in range(GROUPS * BANDS) for b in range(a + 1)]


def overlap_kernel(group_ref, *refs):
    *piece_refs, whole_ref, sums_ref, row_ref = refs
    collect(group_ref[0], piece_refs, whole_ref)

    def accumulate(at, totals):
        cells = [whole_ref[a // BANDS, a % BANDS, at] for a in range(GROUPS * BANDS)]
        return tuple(total + cells[a] * cells[b] for total, (a, b) in zip(totals, PAIRS))

    totals = lax.fori_loop(0, 32, accumulate, tuple(jnp.zeros((8, 128), F32) for _ in PAIRS))
    row_ref[...] = jnp.zeros_like(row_ref)
    for at, total in enumerate(totals):
        row_ref[at : at + 1, :] = jnp.sum(total, axis=0, keepdims=True)
    sums = lax.dot_general(
        jnp.ones((8, 128), F32),
        row_ref[...],
        (((1,), (1,)), ((), ())),
        precision=lax.Precision.HIGHEST,
        preferred_element_type=F32,
    )
    sums_ref[...] = jnp.broadcast_to(sums[0:1].reshape(1, 1, 128), sums_ref.shape)


def rotate_kernel(cell_count, whole_ref, sums_ref, group_ref, *refs):
    *piece_refs, turned_ref = refs
    count = sums_ref.shape[0] // 8
    parts = [jnp.sum(sums_ref[i * count : (i + 1) * count], axis=0) for i in range(8)]
    while len(parts) > 1:
        parts = [parts[i] + parts[i + 1] for i in range(0, len(parts), 2)]
    row = parts[0] * (1.0 / cell_count)
    extent = GROUPS * BANDS
    matrix = {}
    for at, place in enumerate(PAIRS):
        matrix[place] = jnp.broadcast_to(row[:, at : at + 1], (8, 128))
    factor = {}
    scale = []
    for b in range(extent):
        running = matrix[b, b]
        for s in range(b):
            running = running - factor[b, s] * factor[b, s]
        scale.append(1.0 / jnp.sqrt(running))
        for a in range(b + 1, extent):
            running = matrix[a, b]
            for s in range(b):
                running = running - factor[a, s] * factor[b, s]
            factor[a, b] = running * scale[b]
    inverse = {}
    for target in range(extent):
        inverse[target, target] = scale[target]
        for a in range(target):
            running = factor[target, a] * inverse[a, a]
            for source in range(a + 1, target):
                running = running + factor[target, source] * inverse[source, a]
            inverse[target, a] = -running * scale[target]

    def turn(at, carry):
        cells = [whole_ref[a // BANDS, a % BANDS, at] for a in range(extent)]
        for j in range(extent):
            total = inverse[j, 0] * cells[0]
            for a in range(1, j + 1):
                total = total + inverse[j, a] * cells[a]
            turned_ref[j // BANDS, j % BANDS, at] = total
        return carry

    lax.fori_loop(0, 32, turn, 0)
    deal(group_ref[0], turned_ref, piece_refs)


def merge_kernel(group_ref, *refs):
    *piece_refs, out_ref, whole_ref, stage_ref = refs
    collect(group_ref[0], piece_refs, whole_ref)

    def one_band(band, carry):
        for layer in range(LAYERS):
            for v in range(25):
                place = layer * 25 + v
                cell = whole_ref[place // 32, band, place % 32]
                if v < 20:
                    stage_ref[v // 10, pl.ds(v % 10, 8, stride=10), :] = cell
                else:
                    stage_ref[2, pl.ds(v - 20, 8, stride=10), :] = cell
                    stage_ref[2, pl.ds(v - 15, 8, stride=10), :] = pltpu.roll(cell, 64, 1)
            for tile in range(2):
                out_ref[band, layer, :, tile * 128 : tile * 128 + 128] = stage_ref[tile]
            out_ref[band, layer, :, 256:320] = stage_ref[2, :, 0:64]
        return carry

    lax.fori_loop(0, BANDS, one_band, 0)


def shifted(array, axis, step):
    count = lax.axis_size(axis)
    return lax.ppermute(array, axis, [(i, (i + step) % count) for i in range(count)])


def exchange(pieces):
    moved = {step: shifted(pieces[step], "band", step) for step in (2, 1, 3)}
    return [pieces[0], moved[1], moved[2], moved[3]]


def local(band_fields, potential, cutoff, upper_bound):
    smem = pl.BlockSpec(memory_space=pltpu.SMEM)
    vmem = pl.BlockSpec(memory_space=pltpu.VMEM)
    devices = lax.axis_size("dx") * lax.axis_size("dy") * lax.axis_size("band")
    cell_count = float(LAYERS * 80 * 320 * lax.axis_size("dx") * lax.axis_size("dy"))
    group = lax.axis_index("band").astype(jnp.int32).reshape(1)
    state, side_low, side_high, edge_low, edge_high = call(
        split_kernel, (STATE, SIDE, SIDE, EDGE, EDGE), scratch=((3, 80, 128),)
    )(band_fields)
    previous = diagonal = None
    for step in range(4):
        first, last = step == 0, step == 3
        low = shifted(side_high, "dx", 1)
        high = shifted(side_low, "dx", -1)
        below = shifted(edge_high, "dy", 1)
        above = shifted(edge_low, "dy", -1)
        wide = (LAYERS, 3, 18, 8, 128)
        if first:
            part, diagonal = call(
                functools.partial(inner_kernel, True),
                (STATE, STATE[1:]),
                scratch=(wide, (3, 80, 128)),
                in_specs=[vmem, vmem, smem, smem],
            )(state, potential, cutoff, upper_bound)
        else:
            (part,) = call(
                functools.partial(inner_kernel, False), (STATE,), scratch=(wide,), in_specs=[vmem] * 3 + [smem] * 2
            )(state, previous, diagonal, cutoff, upper_bound)
        previous = state
        arguments = (part, low, high, below, above, cutoff, upper_bound)
        in_specs = [vmem] * 5 + [smem] * 2
        rim = (2, 4, 16, 128)
        if last:
            pieces = call(
                functools.partial(outer_kernel, first, last),
                (PIECE,) * 4,
                scratch=((GROUPS,) + PIECE, rim),
                in_specs=in_specs + [smem],
            )(*arguments, group)
        else:
            state, side_low, side_high, edge_low, edge_high = call(
                functools.partial(outer_kernel, first, last),
                (STATE, SIDE, SIDE, EDGE, EDGE),
                scratch=(rim,),
                in_specs=in_specs,
            )(*arguments)
    pieces = exchange(pieces)
    whole, sums = call(
        overlap_kernel,
        ((GROUPS,) + PIECE, (devices, 1, 128)),
        scratch=((128, 128),),
        in_specs=[smem] + [vmem] * 4,
    )(group, *pieces)
    sums = lax.all_to_all(sums, ("dx", "dy", "band"), 0, 0)
    pieces = call(
        functools.partial(rotate_kernel, cell_count),
        (PIECE,) * 4,
        scratch=((GROUPS,) + PIECE,),
        in_specs=[vmem, vmem, smem],
    )(whole, sums, group)
    pieces = exchange(pieces)
    (rotated,) = call(
        merge_kernel,
        ((BANDS, LAYERS, 80, 320),),
        scratch=((GROUPS,) + PIECE, (3, 80, 128)),
        in_specs=[smem] + [vmem] * 4,
    )(group, *pieces)
    return rotated


def solution(mesh):
    in_specs = (P("band", "dx", "dy", None), P("dx", "dy", None), P(), P())
    out_specs = P("band", "dx", "dy", None)
    return jax.shard_map(local, mesh=mesh, in_specs=in_specs, out_specs=out_specs, check_vma=False)
```

```python
import functools

import jax
import jax.numpy as jnp
from jax import lax
from jax.experimental import pallas as pl
from jax.experimental.pallas import tpu as pltpu
from jax.sharding import PartitionSpec as P

BANDS = 2
LAYERS = 5
WIDTH = 4
GROUPS = 4
F32 = jnp.float32

stencil_weights = (-205.0 / 72.0, 8.0 / 5.0, -1.0 / 5.0, 8.0 / 315.0, -1.0 / 560.0)

STATE = (BANDS, LAYERS, 3, 10, 8, 128)
SIDE = (BANDS, WIDTH, 25, 8, 128)
EDGE = (BANDS, 64, 128)
PIECE = (BANDS, 32, 8, 128)


def call(kernel, outs, scratch=(), in_specs=None, cost=4_000_000):
    kwargs = {} if in_specs is None else {"in_specs": in_specs}
    return pl.pallas_call(
        kernel,
        out_shape=tuple(jax.ShapeDtypeStruct(shape, F32) for shape in outs),
        scratch_shapes=[pltpu.VMEM(shape, F32) for shape in scratch],
        compiler_params=pltpu.CompilerParams(vmem_limit_bytes=16 * 1024 * 1024),
        cost_estimate=pl.CostEstimate(flops=cost, bytes_accessed=4_000_000, transcendentals=0),
        **kwargs,
    )


def lanes():
    return lax.broadcasted_iota(jnp.int32, (8, 128), 1)


def sublanes():
    return lax.broadcasted_iota(jnp.int32, (8, 128), 0)


def pair(low, high):
    return jnp.where(lanes() < 64, low, pltpu.roll(high, 64, 1))


def bounds(cutoff_ref, upper_ref):
    low = jnp.broadcast_to(cutoff_ref[...], (8, 128))
    high = jnp.broadcast_to(upper_ref[...], (8, 128))
    return 0.5 * (low + high), 1.0 / (0.5 * (high - low))


def send_sides(tiles, band, layer, low_ref, high_ref):
    for tile in range(2):
        for j in range(10):
            if layer < WIDTH:
                low_ref[band, layer, tile * 10 + j] = tiles[tile][j]
            if layer >= 1:
                high_ref[band, layer - 1, tile * 10 + j] = tiles[tile][j]
    for j in range(5):
        both = pair(tiles[2][j], tiles[2][j + 5])
        if layer < WIDTH:
            low_ref[band, layer, 20 + j] = both
        if layer >= 1:
            high_ref[band, layer - 1, 20 + j] = both


def send_edges(tiles, band, layer, low_ref, high_ref):
    for tile in range(3):
        for j in range(4):
            row = j * 16 + layer * 3 + tile
            low_ref[band, row : row + 1, :] = tiles[tile][j][0:1]
            high_ref[band, row : row + 1, :] = tiles[tile][6 + j][7:8]


def clear_edges(band, *refs):
    for ref in refs:
        for j in range(4):
            ref[band, j * 16 + 15 : j * 16 + 16, :] = jnp.zeros((1, 128), F32)


def parity(axis):
    return lax.rem(lax.axis_index(axis), 2)


def by_parity(axis, body, first, second):
    @pl.when(parity(axis) == 0)
    def even():
        body(first, second)

    @pl.when(parity(axis) == 1)
    def odd():
        body(second, first)


def hand_edges(edge_ref, inner_ref, outer_ref):
    def copy(low_ref, high_ref):
        low_ref[...] = edge_ref[0]
        high_ref[...] = edge_ref[1]

    by_parity("dy", copy, outer_ref, inner_ref)


def split_kernel(field_ref, state_ref, far_ref, near_ref, inner_ref, outer_ref, stage_ref, edge_ref):
    def body(side_low_ref, side_high_ref):
        def one_band(band, carry):
            for layer in range(LAYERS):
                for tile in range(2):
                    stage_ref[tile] = field_ref[band, layer, :, tile * 128 : tile * 128 + 128]
                stage_ref[2, :, 0:64] = field_ref[band, layer, :, 256:320]
                tiles = [[stage_ref[tile, pl.ds(j, 8, stride=10), :] for j in range(10)] for tile in range(3)]
                for tile in range(3):
                    for j in range(10):
                        state_ref[band, layer, tile, j] = tiles[tile][j]
                send_sides(tiles, band, layer, side_low_ref, side_high_ref)
                send_edges(tiles, band, layer, edge_ref.at[0], edge_ref.at[1])
            clear_edges(band, edge_ref.at[0], edge_ref.at[1])
            return carry

        lax.fori_loop(0, BANDS, one_band, 0)

    by_parity("dx", body, far_ref, near_ref)
    hand_edges(edge_ref, inner_ref, outer_ref)


def inner_kernel(first, *refs):
    if first:
        state_ref, potential_ref, cutoff_ref, upper_ref, out_ref, diagonal_ref, wide_ref, stage_ref = refs
    else:
        state_ref, previous_ref, diagonal_ref, cutoff_ref, upper_ref, out_ref, wide_ref = refs
    center, per_half_width = bounds(cutoff_ref, upper_ref)
    if first:
        shift = center + 1.5 * stencil_weights[0]
        for layer in range(LAYERS):
            for tile in range(2):
                stage_ref[tile] = potential_ref[layer, :, tile * 128 : tile * 128 + 128]
            stage_ref[2, :, 0:64] = potential_ref[layer, :, 256:320]
            for tile in range(3):
                for j in range(10):
                    cells = stage_ref[tile, pl.ds(j, 8, stride=10), :]
                    diagonal_ref[layer, tile, j] = 2.0 * ((cells - shift) * per_half_width)
    factor = 1.0 if first else 2.0
    weights = [None] + [(-0.5 * factor * stencil_weights[k]) * per_half_width for k in range(1, 5)]
    lane = lanes()
    row = sublanes()

    def one_band(band, carry):
        def widen(j, carry):
            for layer in range(LAYERS):
                tiles = [state_ref[band, layer, tile, j] for tile in range(3)]
                tiles[2] = jnp.where(
                    lane < 64,
                    tiles[2],
                    jnp.where(lane < 96, pltpu.roll(tiles[0], 64, 1), pltpu.roll(tiles[2], 64, 1)),
                )
                for tile in range(3):
                    wide_ref[layer, tile, j + 4] = tiles[tile]
            return carry

        lax.fori_loop(0, 10, widen, 0)

        def wrap(j, carry):
            for layer in range(LAYERS):
                for tile in range(3):
                    above = wide_ref[layer, tile, j + 4]
                    wide_ref[layer, tile, j + 14] = jnp.where(row < 7, pltpu.roll(above, 7, 0), 0.0)
                    below = wide_ref[layer, tile, j + 10]
                    wide_ref[layer, tile, j] = jnp.where(row > 0, pltpu.roll(below, 1, 0), 0.0)
            return carry

        lax.fori_loop(0, 4, wrap, 0)

        def rows(j, carry):
            mids = [[wide_ref[layer, tile, j + 4] for tile in range(3)] for layer in range(LAYERS)]
            for layer in range(LAYERS):
                mid = mids[layer]
                lefts = [pltpu.roll(mid[tile], 1, 1) for tile in range(3)]
                lefts = [jnp.where(lane < 1, lefts[(tile + 2) % 3], lefts[tile]) for tile in range(3)]
                rights = [pltpu.roll(mid[tile], 127, 1) for tile in range(3)]
                rights = [jnp.where(lane < 127, rights[tile], rights[(tile + 1) % 3]) for tile in range(3)]
                ups, downs = [], []
                for tile in range(3):
                    centre = weights[3] * mid[tile]
                    ups.append(centre + weights[2] * lefts[tile] + weights[4] * rights[tile])
                    downs.append(centre + weights[4] * lefts[tile] + weights[2] * rights[tile])
                ups = [pltpu.roll(up, 125, 1) for up in ups]
                downs = [pltpu.roll(down, 3, 1) for down in downs]
                for tile in range(3):
                    up = ups[2] if tile == 2 else jnp.where(lane < 125, ups[tile], ups[tile + 1])
                    total = up + jnp.where(lane < 3, downs[(tile + 2) % 3], downs[tile])
                    for k in range(1, 5):
                        part = wide_ref[layer, tile, j + 4 + k] + wide_ref[layer, tile, j + 4 - k]
                        if k == 1:
                            part += lefts[tile] + rights[tile]
                        if layer + k < LAYERS:
                            part += mids[layer + k][tile]
                        if layer - k >= 0:
                            part += mids[layer - k][tile]
                        total += weights[k] * part
                    diagonal = diagonal_ref[layer, tile, j] * mid[tile]
                    if first:
                        out_ref[band, layer, tile, j] = total + 0.5 * diagonal
                    else:
                        out_ref[band, layer, tile, j] = total + (diagonal - previous_ref[band, layer, tile, j])
            return carry

        return lax.fori_loop(0, 10, rows, carry)

    lax.fori_loop(0, BANDS, one_band, 0)


def outer_kernel(first, last, *refs):
    part_ref, far_in_ref, near_in_ref, inner_in_ref, outer_in_ref, cutoff_ref, upper_ref, *refs = refs
    if last:
        *piece_refs, rim_ref, whole_ref = refs
        state_ref, far_ref, near_ref, edge_ref = None, None, None, None
    else:
        state_ref, far_ref, near_ref, inner_ref, outer_ref, rim_ref, edge_ref = refs
        whole_ref = None
    _, per_half_width = bounds(cutoff_ref, upper_ref)
    factor = 1.0 if first else 2.0
    weights = [None] + [(-0.5 * factor * stencil_weights[k]) * per_half_width for k in range(1, 5)]

    def rims(below_ref, above_ref):
        def one_band(band, carry):
            for half in range(2):
                below = [below_ref[band, 16 * j + 8 * half : 16 * j + 8 * half + 8, :] for j in range(4)]
                above = [above_ref[band, 16 * j + 8 * half : 16 * j + 8 * half + 8, :] for j in range(4)]
                for j in range(4):
                    rim_ref[band, 0, j, 8 * half : 8 * half + 8, :] = sum(
                        weights[k] * below[4 + j - k] for k in range(j + 1, 5)
                    )
                    rim_ref[band, 1, j, 8 * half : 8 * half + 8, :] = sum(
                        weights[k] * above[j + 6 + k - 10] for k in range(4 - j, 5)
                    )
            return carry

        lax.fori_loop(0, BANDS, one_band, 0)

    by_parity("dy", rims, outer_in_ref, inner_in_ref)

    def body(low, high):
        add_outside(weights, part_ref, rim_ref, low, high, state_ref, edge_ref, whole_ref)

    by_parity("dx", body, (far_in_ref, far_ref), (near_in_ref, near_ref))
    if last:
        deal(whole_ref, piece_refs)
    else:
        hand_edges(edge_ref, inner_ref, outer_ref)


def add_outside(weights, part_ref, rim_ref, low, high, state_ref, edge_ref, whole_ref):
    low_ref, side_low_ref = low
    high_ref, side_high_ref = high
    last = whole_ref is not None
    row = sublanes()

    def one_band(band, carry):
        for layer in range(LAYERS):
            outside = []
            for v in range(25):
                terms = [weights[layer + 4 - i] * low_ref[band, i, v] for i in range(layer, 4)]
                terms += [weights[5 + i - layer] * high_ref[band, i, v] for i in range(layer)]
                outside.append((terms[0] + terms[1]) + (terms[2] + terms[3]))
            tiles = []
            for tile in range(3):
                cells = []
                for j in range(10):
                    if tile < 2:
                        extra = outside[tile * 10 + j]
                    elif j < 5:
                        extra = outside[20 + j]
                    else:
                        extra = pltpu.roll(outside[15 + j], 64, 1)
                    cell = part_ref[band, layer, tile, j] + extra
                    at = layer * 3 + tile
                    if j < 4:
                        cell += jnp.where(row == 0, rim_ref[band, 0, j, at : at + 1, :], 0.0)
                    if j >= 6:
                        cell += jnp.where(row == 7, rim_ref[band, 1, j - 6, at : at + 1, :], 0.0)
                    cells.append(cell)
                tiles.append(cells)
            if last:
                packed = tiles[0] + tiles[1] + [pair(tiles[2][j], tiles[2][j + 5]) for j in range(5)]
                for v in range(25):
                    place = layer * 25 + v
                    whole_ref[place // 32, band, place % 32] = packed[v]
            else:
                for tile in range(3):
                    for j in range(10):
                        state_ref[band, layer, tile, j] = tiles[tile][j]
                send_sides(tiles, band, layer, side_low_ref, side_high_ref)
                send_edges(tiles, band, layer, edge_ref.at[0], edge_ref.at[1])
        if last:
            for place in range(125, 128):
                whole_ref[place // 32, band, place % 32] = jnp.zeros((8, 128), F32)
        else:
            clear_edges(band, edge_ref.at[0], edge_ref.at[1])
        return carry

    lax.fori_loop(0, BANDS, one_band, 0)


def deal(whole_ref, piece_refs):
    for step, piece_ref in enumerate(piece_refs):
        piece_ref[...] = whole_ref[lax.axis_index("band") ^ step]


def collect(piece_refs, whole_ref):
    for step, piece_ref in enumerate(piece_refs):
        whole_ref[lax.axis_index("band") ^ step] = piece_ref[...]


PAIRS = [(a, b) for a in range(GROUPS * BANDS) for b in range(a + 1)]


def overlap_kernel(*refs):
    *piece_refs, whole_ref, sums_ref, row_ref = refs
    collect(piece_refs, whole_ref)

    def accumulate(at, totals):
        cells = [whole_ref[a // BANDS, a % BANDS, at] for a in range(GROUPS * BANDS)]
        return tuple(total + cells[a] * cells[b] for total, (a, b) in zip(totals, PAIRS))

    totals = lax.fori_loop(0, 32, accumulate, tuple(jnp.zeros((8, 128), F32) for _ in PAIRS))
    row_ref[...] = jnp.zeros_like(row_ref)
    for at, total in enumerate(totals):
        row_ref[at : at + 1, :] = jnp.sum(total, axis=0, keepdims=True)
    sums = lax.dot_general(
        jnp.ones((8, 128), F32),
        row_ref[...],
        (((1,), (1,)), ((), ())),
        precision=lax.Precision.HIGHEST,
        preferred_element_type=F32,
    )
    sums_ref[...] = jnp.broadcast_to(sums[0:1].reshape(1, 1, 128), sums_ref.shape)


def rotate_kernel(cell_count, whole_ref, sums_ref, *refs):
    *piece_refs, turned_ref = refs
    count = sums_ref.shape[0] // 8
    parts = [jnp.sum(sums_ref[i * count : (i + 1) * count], axis=0) for i in range(8)]
    while len(parts) > 1:
        parts = [parts[i] + parts[i + 1] for i in range(0, len(parts), 2)]
    row = parts[0] * (1.0 / cell_count)
    extent = GROUPS * BANDS
    matrix = {}
    for at, place in enumerate(PAIRS):
        matrix[place] = jnp.broadcast_to(row[:, at : at + 1], (8, 128))
    factor = {}
    scale = []
    for b in range(extent):
        running = matrix[b, b]
        for s in range(b):
            running = running - factor[b, s] * factor[b, s]
        scale.append(1.0 / jnp.sqrt(running))
        for a in range(b + 1, extent):
            running = matrix[a, b]
            for s in range(b):
                running = running - factor[a, s] * factor[b, s]
            factor[a, b] = running * scale[b]
    inverse = {}
    for target in range(extent):
        inverse[target, target] = scale[target]
        for a in range(target):
            running = factor[target, a] * inverse[a, a]
            for source in range(a + 1, target):
                running = running + factor[target, source] * inverse[source, a]
            inverse[target, a] = -running * scale[target]

    def turn(at, carry):
        cells = [whole_ref[a // BANDS, a % BANDS, at] for a in range(extent)]
        for j in range(extent):
            total = inverse[j, 0] * cells[0]
            for a in range(1, j + 1):
                total = total + inverse[j, a] * cells[a]
            turned_ref[j // BANDS, j % BANDS, at] = total
        return carry

    lax.fori_loop(0, 32, turn, 0)
    deal(turned_ref, piece_refs)


def merge_kernel(*refs):
    *piece_refs, out_ref, whole_ref, stage_ref = refs
    collect(piece_refs, whole_ref)

    def one_band(band, carry):
        for layer in range(LAYERS):
            for v in range(25):
                place = layer * 25 + v
                cell = whole_ref[place // 32, band, place % 32]
                if v < 20:
                    stage_ref[v // 10, pl.ds(v % 10, 8, stride=10), :] = cell
                else:
                    stage_ref[2, pl.ds(v - 20, 8, stride=10), :] = cell
                    stage_ref[2, pl.ds(v - 15, 8, stride=10), :] = pltpu.roll(cell, 64, 1)
            for tile in range(2):
                out_ref[band, layer, :, tile * 128 : tile * 128 + 128] = stage_ref[tile]
            out_ref[band, layer, :, 256:320] = stage_ref[2, :, 0:64]
        return carry

    lax.fori_loop(0, BANDS, one_band, 0)


def swapped(array, axis, partner):
    return lax.ppermute(array, axis, [(i, partner(i)) for i in range(lax.axis_size(axis))])


def beside(array, axis, offset):
    count = lax.axis_size(axis)
    return swapped(array, axis, lambda i: (i + (offset if i % 2 == 0 else -offset)) % count)


def exchange(pieces):
    moved = {step: swapped(pieces[step], "band", lambda i: i ^ step) for step in (2, 1, 3)}
    return [pieces[0], moved[1], moved[2], moved[3]]


def local(band_fields, potential, cutoff, upper_bound):
    devices = lax.axis_size("dx") * lax.axis_size("dy") * lax.axis_size("band")
    cell_count = float(LAYERS * 80 * 320 * lax.axis_size("dx") * lax.axis_size("dy"))
    cutoff = cutoff.reshape(1, 1)
    upper_bound = upper_bound.reshape(1, 1)
    stage = (3, 80, 128)
    edges = (2,) + EDGE
    state, far, near, inner, outer = call(
        split_kernel, (STATE, SIDE, SIDE, EDGE, EDGE), scratch=(stage, edges)
    )(band_fields)
    previous = diagonal = None
    for step in range(4):
        first, last = step == 0, step == 3
        far = beside(far, "dx", -1)
        near = beside(near, "dx", 1)
        inner = beside(inner, "dy", 1)
        outer = beside(outer, "dy", -1)
        wide = (LAYERS, 3, 18, 8, 128)
        if first:
            part, diagonal = call(
                functools.partial(inner_kernel, True), (STATE, STATE[1:]), scratch=(wide, stage)
            )(state, potential, cutoff, upper_bound)
        else:
            (part,) = call(functools.partial(inner_kernel, False), (STATE,), scratch=(wide,))(
                state, previous, diagonal, cutoff, upper_bound
            )
        previous = state
        arguments = (part, far, near, inner, outer, cutoff, upper_bound)
        rim = (BANDS, 2, 4, 16, 128)
        if last:
            pieces = call(
                functools.partial(outer_kernel, first, last),
                (PIECE,) * 4,
                scratch=(rim, (GROUPS,) + PIECE),
            )(*arguments)
        else:
            state, far, near, inner, outer = call(
                functools.partial(outer_kernel, first, last),
                (STATE, SIDE, SIDE, EDGE, EDGE),
                scratch=(rim, edges),
            )(*arguments)
    pieces = exchange(pieces)
    whole, sums = call(overlap_kernel, ((GROUPS,) + PIECE, (devices, 1, 128)), scratch=((128, 128),))(*pieces)
    sums = lax.all_to_all(sums, ("dx", "dy", "band"), 0, 0)
    pieces = call(
        functools.partial(rotate_kernel, cell_count), (PIECE,) * 4, scratch=((GROUPS,) + PIECE,)
    )(whole, sums)
    pieces = exchange(pieces)
    (rotated,) = call(
        merge_kernel, ((BANDS, LAYERS, 80, 320),), scratch=((GROUPS,) + PIECE, stage)
    )(*pieces)
    return rotated


def solution(mesh):
    in_specs = (P("band", "dx", "dy", None), P("dx", "dy", None), P(), P())
    out_specs = P("band", "dx", "dy", None)
    return jax.shard_map(local, mesh=mesh, in_specs=in_specs, out_specs=out_specs, check_vma=False)
```

```python
import functools

import jax
import jax.numpy as jnp
from jax import lax
from jax.experimental import pallas as pl
from jax.experimental.pallas import tpu as pltpu
from jax.sharding import PartitionSpec as P

BANDS = 2
LAYERS = 5
WIDTH = 4
GROUPS = 4
F32 = jnp.float32

stencil_weights = (-205.0 / 72.0, 8.0 / 5.0, -1.0 / 5.0, 8.0 / 315.0, -1.0 / 560.0)

STATE = (BANDS, LAYERS, 3, 10, 8, 128)
SIDE = (BANDS, WIDTH, 25, 8, 128)
EDGE = (BANDS, 64, 128)
PIECE = (BANDS, 32, 8, 128)


def call(kernel, outs, scratch=(), semaphores=0, **kwargs):
    scratch = [pltpu.VMEM(shape, F32) for shape in scratch]
    if semaphores:
        scratch.append(pltpu.SemaphoreType.DMA((semaphores,)))
    return pl.pallas_call(
        kernel,
        out_shape=tuple(jax.ShapeDtypeStruct(shape, F32) for shape in outs),
        scratch_shapes=scratch,
        compiler_params=pltpu.CompilerParams(vmem_limit_bytes=16 * 1024 * 1024),
        cost_estimate=pl.CostEstimate(flops=4_000_000, bytes_accessed=4_000_000, transcendentals=0),
        **kwargs,
    )


def lanes():
    return lax.broadcasted_iota(jnp.int32, (8, 128), 1)


def sublanes():
    return lax.broadcasted_iota(jnp.int32, (8, 128), 0)


def pair(low, high):
    return jnp.where(lanes() < 64, low, pltpu.roll(high, 64, 1))


def bounds(cutoff_ref, upper_ref):
    low = jnp.broadcast_to(cutoff_ref[...], (8, 128))
    high = jnp.broadcast_to(upper_ref[...], (8, 128))
    return 0.5 * (low + high), 1.0 / (0.5 * (high - low))


def send_sides(tiles, band, layer, low_ref, high_ref):
    for tile in range(2):
        for j in range(10):
            if layer < WIDTH:
                low_ref[band, layer, tile * 10 + j] = tiles[tile][j]
            if layer >= 1:
                high_ref[band, layer - 1, tile * 10 + j] = tiles[tile][j]
    for j in range(5):
        both = pair(tiles[2][j], tiles[2][j + 5])
        if layer < WIDTH:
            low_ref[band, layer, 20 + j] = both
        if layer >= 1:
            high_ref[band, layer - 1, 20 + j] = both


def send_edges(tiles, band, layer, low_ref, high_ref):
    for tile in range(3):
        for j in range(4):
            row = j * 16 + layer * 3 + tile
            low_ref[band, row : row + 1, :] = tiles[tile][j][0:1]
            high_ref[band, row : row + 1, :] = tiles[tile][6 + j][7:8]


def clear_edges(band, *refs):
    for ref in refs:
        for j in range(4):
            ref[band, j * 16 + 15 : j * 16 + 16, :] = jnp.zeros((1, 128), F32)


def parity(axis):
    return lax.rem(lax.axis_index(axis), 2)


def by_parity(axis, body, first, second):
    @pl.when(parity(axis) == 0)
    def even():
        body(first, second)

    @pl.when(parity(axis) == 1)
    def odd():
        body(second, first)


def hand_edges(edge_ref, inner_ref, outer_ref):
    def copy(low_ref, high_ref):
        low_ref[...] = edge_ref[0]
        high_ref[...] = edge_ref[1]

    by_parity("dy", copy, outer_ref, inner_ref)


def split_kernel(field_ref, state_ref, far_ref, near_ref, inner_ref, outer_ref, stage_ref, edge_ref):
    def body(side_low_ref, side_high_ref):
        def one_band(band, carry):
            for layer in range(LAYERS):
                for tile in range(2):
                    stage_ref[tile] = field_ref[band, layer, :, tile * 128 : tile * 128 + 128]
                stage_ref[2, :, 0:64] = field_ref[band, layer, :, 256:320]
                tiles = [[stage_ref[tile, pl.ds(j, 8, stride=10), :] for j in range(10)] for tile in range(3)]
                for tile in range(3):
                    for j in range(10):
                        state_ref[band, layer, tile, j] = tiles[tile][j]
                send_sides(tiles, band, layer, side_low_ref, side_high_ref)
                send_edges(tiles, band, layer, edge_ref.at[0], edge_ref.at[1])
            clear_edges(band, edge_ref.at[0], edge_ref.at[1])
            return carry

        lax.fori_loop(0, BANDS, one_band, 0)

    by_parity("dx", body, far_ref, near_ref)
    hand_edges(edge_ref, inner_ref, outer_ref)


def inner_kernel(first, *refs):
    if first:
        state_ref, potential_ref, cutoff_ref, upper_ref, out_ref, diagonal_ref, wide_ref, stage_ref = refs
    else:
        state_ref, previous_ref, diagonal_ref, cutoff_ref, upper_ref, out_ref, wide_ref = refs
    center, per_half_width = bounds(cutoff_ref, upper_ref)
    if first:
        shift = center + 1.5 * stencil_weights[0]
        for layer in range(LAYERS):
            for tile in range(2):
                stage_ref[tile] = potential_ref[layer, :, tile * 128 : tile * 128 + 128]
            stage_ref[2, :, 0:64] = potential_ref[layer, :, 256:320]
            for tile in range(3):
                for j in range(10):
                    cells = stage_ref[tile, pl.ds(j, 8, stride=10), :]
                    diagonal_ref[layer, tile, j] = 2.0 * ((cells - shift) * per_half_width)
    factor = 1.0 if first else 2.0
    weights = [None] + [(-0.5 * factor * stencil_weights[k]) * per_half_width for k in range(1, 5)]
    lane = lanes()
    row = sublanes()

    def plane(at, carry):
        band, layer = at // LAYERS, lax.rem(at, LAYERS)
        for j in range(10):
            tiles = [state_ref[band, layer, tile, j] for tile in range(3)]
            tiles[2] = jnp.where(
                lane < 64, tiles[2], jnp.where(lane < 96, pltpu.roll(tiles[0], 64, 1), pltpu.roll(tiles[2], 64, 1))
            )
            for tile in range(3):
                wide_ref[tile, j] = tiles[tile]
        for tile in range(3):
            ext = [wide_ref[tile, j] for j in range(10)]
            below = [jnp.where(row > 0, pltpu.roll(cells, 1, 0), 0.0) for cells in ext[6:]]
            above = [jnp.where(row < 7, pltpu.roll(cells, 7, 0), 0.0) for cells in ext[:4]]
            ext = below + ext + above
            for j in range(10):
                total = None
                for k in range(1, 5):
                    part = weights[k] * (ext[j + 4 + k] + ext[j + 4 - k])
                    total = part if total is None else total + part
                out_ref[band, layer, tile, j] = total
        for j in range(10):
            mid = [wide_ref[tile, j] for tile in range(3)]
            lefts = [pltpu.roll(cells, 1, 1) for cells in mid]
            lefts = [jnp.where(lane < 1, lefts[(tile + 2) % 3], lefts[tile]) for tile in range(3)]
            rights = [pltpu.roll(cells, 127, 1) for cells in mid]
            rights = [jnp.where(lane < 127, rights[tile], rights[(tile + 1) % 3]) for tile in range(3)]
            ups, downs = [], []
            for tile in range(3):
                centre = weights[3] * mid[tile]
                ups.append(centre + weights[2] * lefts[tile] + weights[4] * rights[tile])
                downs.append(centre + weights[4] * lefts[tile] + weights[2] * rights[tile])
            ups = [pltpu.roll(up, 125, 1) for up in ups]
            downs = [pltpu.roll(down, 3, 1) for down in downs]
            for tile in range(3):
                up = ups[2] if tile == 2 else jnp.where(lane < 125, ups[tile], ups[tile + 1])
                total = up + jnp.where(lane < 3, downs[(tile + 2) % 3], downs[tile])
                total += weights[1] * (lefts[tile] + rights[tile])
                out_ref[band, layer, tile, j] += total
        return carry

    lax.fori_loop(0, BANDS * LAYERS, plane, 0)

    def column(at, carry):
        band, j = at // 10, lax.rem(at, 10)
        for tile in range(3):
            mids = [state_ref[band, layer, tile, j] for layer in range(LAYERS)]
            for layer in range(LAYERS):
                total = out_ref[band, layer, tile, j]
                for k in range(1, 5):
                    near = [mids[at] for at in (layer - k, layer + k) if 0 <= at < LAYERS]
                    if near:
                        total += weights[k] * sum(near[1:], near[0])
                diagonal = diagonal_ref[layer, tile, j] * mids[layer]
                if first:
                    out_ref[band, layer, tile, j] = total + 0.5 * diagonal
                else:
                    out_ref[band, layer, tile, j] = total + (diagonal - previous_ref[band, layer, tile, j])
        return carry

    lax.fori_loop(0, BANDS * 10, column, 0)


def outer_kernel(first, last, *refs):
    part_ref, far_in_ref, near_in_ref, inner_in_ref, outer_in_ref, cutoff_ref, upper_ref, *refs = refs
    if last:
        *piece_refs, rim_ref, whole_ref = refs
        state_ref, far_ref, near_ref, edge_ref = None, None, None, None
    else:
        state_ref, far_ref, near_ref, inner_ref, outer_ref, rim_ref, edge_ref = refs
        whole_ref = None
    _, per_half_width = bounds(cutoff_ref, upper_ref)
    factor = 1.0 if first else 2.0
    weights = [None] + [(-0.5 * factor * stencil_weights[k]) * per_half_width for k in range(1, 5)]

    def rims(below_ref, above_ref):
        def one_band(band, carry):
            for half in range(2):
                below = [below_ref[band, 16 * j + 8 * half : 16 * j + 8 * half + 8, :] for j in range(4)]
                above = [above_ref[band, 16 * j + 8 * half : 16 * j + 8 * half + 8, :] for j in range(4)]
                for j in range(4):
                    rim_ref[band, 0, j, 8 * half : 8 * half + 8, :] = sum(
                        weights[k] * below[4 + j - k] for k in range(j + 1, 5)
                    )
                    rim_ref[band, 1, j, 8 * half : 8 * half + 8, :] = sum(
                        weights[k] * above[j + 6 + k - 10] for k in range(4 - j, 5)
                    )
            return carry

        lax.fori_loop(0, BANDS, one_band, 0)

    by_parity("dy", rims, outer_in_ref, inner_in_ref)

    def body(low, high):
        add_outside(weights, part_ref, rim_ref, low, high, state_ref, edge_ref, whole_ref)

    by_parity("dx", body, (far_in_ref, far_ref), (near_in_ref, near_ref))
    if last:
        deal(whole_ref, piece_refs)
    else:
        hand_edges(edge_ref, inner_ref, outer_ref)


def add_outside(weights, part_ref, rim_ref, low, high, state_ref, edge_ref, whole_ref):
    low_ref, side_low_ref = low
    high_ref, side_high_ref = high
    last = whole_ref is not None
    row = sublanes()

    def one_band(band, carry):
        for layer in range(LAYERS):
            outside = []
            for v in range(25):
                terms = [weights[layer + 4 - i] * low_ref[band, i, v] for i in range(layer, 4)]
                terms += [weights[5 + i - layer] * high_ref[band, i, v] for i in range(layer)]
                outside.append((terms[0] + terms[1]) + (terms[2] + terms[3]))
            tiles = []
            for tile in range(3):
                cells = []
                for j in range(10):
                    if tile < 2:
                        extra = outside[tile * 10 + j]
                    elif j < 5:
                        extra = outside[20 + j]
                    else:
                        extra = pltpu.roll(outside[15 + j], 64, 1)
                    cell = part_ref[band, layer, tile, j] + extra
                    at = layer * 3 + tile
                    if j < 4:
                        cell += jnp.where(row == 0, rim_ref[band, 0, j, at : at + 1, :], 0.0)
                    if j >= 6:
                        cell += jnp.where(row == 7, rim_ref[band, 1, j - 6, at : at + 1, :], 0.0)
                    cells.append(cell)
                tiles.append(cells)
            if last:
                packed = tiles[0] + tiles[1] + [pair(tiles[2][j], tiles[2][j + 5]) for j in range(5)]
                for v in range(25):
                    place = layer * 25 + v
                    whole_ref[place // 32, band, place % 32] = packed[v]
            else:
                for tile in range(3):
                    for j in range(10):
                        state_ref[band, layer, tile, j] = tiles[tile][j]
                send_sides(tiles, band, layer, side_low_ref, side_high_ref)
                send_edges(tiles, band, layer, edge_ref.at[0], edge_ref.at[1])
        if last:
            for place in range(125, 128):
                whole_ref[place // 32, band, place % 32] = jnp.zeros((8, 128), F32)
        else:
            clear_edges(band, edge_ref.at[0], edge_ref.at[1])
        return carry

    lax.fori_loop(0, BANDS, one_band, 0)


def deal(whole_ref, piece_refs):
    for step, piece_ref in enumerate(piece_refs):
        piece_ref[...] = whole_ref[lax.axis_index("band") ^ step]


def collect(piece_refs, whole_ref):
    for step, piece_ref in enumerate(piece_refs):
        whole_ref[lax.axis_index("band") ^ step] = piece_ref[...]


PAIRS = [(a, b) for a in range(GROUPS * BANDS) for b in range(a + 1)]


def overlap_kernel(*refs):
    *piece_refs, whole_ref, sums_ref, row_ref = refs
    collect(piece_refs, whole_ref)

    def accumulate(at, totals):
        cells = [whole_ref[a // BANDS, a % BANDS, at] for a in range(GROUPS * BANDS)]
        return tuple(total + cells[a] * cells[b] for total, (a, b) in zip(totals, PAIRS))

    totals = lax.fori_loop(0, 32, accumulate, tuple(jnp.zeros((8, 128), F32) for _ in PAIRS))
    row_ref[...] = jnp.zeros_like(row_ref)
    for at, total in enumerate(totals):
        row_ref[at : at + 1, :] = jnp.sum(total, axis=0, keepdims=True)
    sums = lax.dot_general(
        jnp.ones((8, 128), F32),
        row_ref[...],
        (((1,), (1,)), ((), ())),
        precision=lax.Precision.HIGHEST,
        preferred_element_type=F32,
    )
    sums_ref[...] = jnp.broadcast_to(sums[0:1].reshape(1, 1, 128), sums_ref.shape)


def rotate_kernel(cell_count, whole_ref, sums_ref, *refs):
    *piece_refs, turned_ref = refs
    count = sums_ref.shape[0] // 8
    parts = [jnp.sum(sums_ref[i * count : (i + 1) * count], axis=0) for i in range(8)]
    while len(parts) > 1:
        parts = [parts[i] + parts[i + 1] for i in range(0, len(parts), 2)]
    row = parts[0] * (1.0 / cell_count)
    extent = GROUPS * BANDS
    matrix = {}
    for at, place in enumerate(PAIRS):
        matrix[place] = jnp.broadcast_to(row[:, at : at + 1], (8, 128))
    factor = {}
    scale = []
    for b in range(extent):
        running = matrix[b, b]
        for s in range(b):
            running = running - factor[b, s] * factor[b, s]
        scale.append(1.0 / jnp.sqrt(running))
        for a in range(b + 1, extent):
            running = matrix[a, b]
            for s in range(b):
                running = running - factor[a, s] * factor[b, s]
            factor[a, b] = running * scale[b]
    inverse = {}
    for target in range(extent):
        inverse[target, target] = scale[target]
        for a in range(target):
            running = factor[target, a] * inverse[a, a]
            for source in range(a + 1, target):
                running = running + factor[target, source] * inverse[source, a]
            inverse[target, a] = -running * scale[target]

    def turn(at, carry):
        cells = [whole_ref[a // BANDS, a % BANDS, at] for a in range(extent)]
        for j in range(extent):
            total = inverse[j, 0] * cells[0]
            for a in range(1, j + 1):
                total = total + inverse[j, a] * cells[a]
            turned_ref[j // BANDS, j % BANDS, at] = total
        return carry

    lax.fori_loop(0, 32, turn, 0)
    deal(turned_ref, piece_refs)


def merge_kernel(*refs):
    *piece_refs, out_ref, whole_ref, stage_ref, plane_ref, sems = refs
    collect(piece_refs, whole_ref)

    def copy_out(at):
        return pltpu.make_async_copy(plane_ref.at[at], out_ref.at[at // LAYERS, at % LAYERS], sems.at[at])

    for at in range(BANDS * LAYERS):
        band, layer = at // LAYERS, at % LAYERS
        for v in range(25):
            place = layer * 25 + v
            cell = whole_ref[place // 32, band, place % 32]
            if v < 20:
                stage_ref[v // 10, pl.ds(v % 10, 8, stride=10), :] = cell
            else:
                stage_ref[2, pl.ds(v - 20, 8, stride=10), :] = cell
                stage_ref[2, pl.ds(v - 15, 8, stride=10), :] = pltpu.roll(cell, 64, 1)
        for tile in range(2):
            plane_ref[at, :, tile * 128 : tile * 128 + 128] = stage_ref[tile]
        plane_ref[at, :, 256:320] = stage_ref[2, :, 0:64]
        copy_out(at).start()
    for at in range(BANDS * LAYERS):
        copy_out(at).wait()


def swapped(array, axis, partner):
    return lax.ppermute(array, axis, [(i, partner(i)) for i in range(lax.axis_size(axis))])


def beside(array, axis, offset):
    count = lax.axis_size(axis)
    return swapped(array, axis, lambda i: (i + (offset if i % 2 == 0 else -offset)) % count)


def exchange(pieces):
    moved = {step: swapped(pieces[step], "band", lambda i: i ^ step) for step in (2, 1, 3)}
    return [pieces[0], moved[1], moved[2], moved[3]]


def local(band_fields, potential, cutoff, upper_bound):
    devices = lax.axis_size("dx") * lax.axis_size("dy") * lax.axis_size("band")
    cell_count = float(LAYERS * 80 * 320 * lax.axis_size("dx") * lax.axis_size("dy"))
    cutoff = cutoff.reshape(1, 1)
    upper_bound = upper_bound.reshape(1, 1)
    stage = (3, 80, 128)
    edges = (2,) + EDGE
    state, far, near, inner, outer = call(
        split_kernel, (STATE, SIDE, SIDE, EDGE, EDGE), scratch=(stage, edges)
    )(band_fields)
    previous = diagonal = None
    for step in range(4):
        first, last = step == 0, step == 3
        far = beside(far, "dx", -1)
        near = beside(near, "dx", 1)
        inner = beside(inner, "dy", 1)
        outer = beside(outer, "dy", -1)
        wide = (3, 10, 8, 128)
        if first:
            part, diagonal = call(
                functools.partial(inner_kernel, True), (STATE, STATE[1:]), scratch=(wide, stage)
            )(state, potential, cutoff, upper_bound)
        else:
            (part,) = call(functools.partial(inner_kernel, False), (STATE,), scratch=(wide,))(
                state, previous, diagonal, cutoff, upper_bound
            )
        previous = state
        arguments = (part, far, near, inner, outer, cutoff, upper_bound)
        rim = (BANDS, 2, 4, 16, 128)
        if last:
            pieces = call(
                functools.partial(outer_kernel, first, last),
                (PIECE,) * 4,
                scratch=(rim, (GROUPS,) + PIECE),
            )(*arguments)
        else:
            state, far, near, inner, outer = call(
                functools.partial(outer_kernel, first, last),
                (STATE, SIDE, SIDE, EDGE, EDGE),
                scratch=(rim, edges),
            )(*arguments)
    pieces = exchange(pieces)
    whole, sums = call(overlap_kernel, ((GROUPS,) + PIECE, (devices, 1, 128)), scratch=((128, 128),))(*pieces)
    sums = lax.all_to_all(sums, ("dx", "dy", "band"), 0, 0)
    pieces = call(
        functools.partial(rotate_kernel, cell_count), (PIECE,) * 4, scratch=((GROUPS,) + PIECE,)
    )(whole, sums)
    pieces = exchange(pieces)
    planes = BANDS * LAYERS
    (rotated,) = call(
        merge_kernel,
        ((BANDS, LAYERS, 80, 320),),
        scratch=((GROUPS,) + PIECE, stage, (planes, 80, 320)),
        semaphores=planes,
        out_specs=(pl.BlockSpec(memory_space=pl.ANY),),
    )(*pieces)
    return rotated


def solution(mesh):
    in_specs = (P("band", "dx", "dy", None), P("dx", "dy", None), P(), P())
    out_specs = P("band", "dx", "dy", None)
    return jax.shard_map(local, mesh=mesh, in_specs=in_specs, out_specs=out_specs, check_vma=False)
```

```python
import functools

import jax
import jax.numpy as jnp
from jax import lax
from jax.experimental import pallas as pl
from jax.experimental.pallas import tpu as pltpu
from jax.sharding import PartitionSpec as P

BANDS = 2
LAYERS = 5
WIDTH = 4
GROUPS = 4
F32 = jnp.float32

stencil_weights = (-205.0 / 72.0, 8.0 / 5.0, -1.0 / 5.0, 8.0 / 315.0, -1.0 / 560.0)

STATE = (BANDS, LAYERS, 3, 10, 8, 128)
SIDE = (BANDS, WIDTH, 25, 8, 128)
EDGE = (104, 128)
EDGE_ROWS = 50
WHOLE = (GROUPS, BANDS, 32, 8, 128)


def call(kernel, outs, scratch=(), semaphores=0, **kwargs):
    scratch = [pltpu.VMEM(shape, F32) for shape in scratch]
    if semaphores:
        scratch.append(pltpu.SemaphoreType.DMA((semaphores,)))
    return pl.pallas_call(
        kernel,
        out_shape=tuple(jax.ShapeDtypeStruct(shape, F32) for shape in outs),
        scratch_shapes=scratch,
        compiler_params=pltpu.CompilerParams(vmem_limit_bytes=16 * 1024 * 1024),
        cost_estimate=pl.CostEstimate(flops=4_000_000, bytes_accessed=4_000_000, transcendentals=0),
        **kwargs,
    )


def lanes():
    return lax.broadcasted_iota(jnp.int32, (8, 128), 1)


def sublanes():
    return lax.broadcasted_iota(jnp.int32, (8, 128), 0)


def pair(low, high):
    return jnp.where(lanes() < 64, low, pltpu.roll(high, 64, 1))


def bounds(cutoff_ref, upper_ref):
    low = jnp.broadcast_to(cutoff_ref[...], (8, 128))
    high = jnp.broadcast_to(upper_ref[...], (8, 128))
    return 0.5 * (low + high), 1.0 / (0.5 * (high - low))


def send_sides(tiles, band, layer, low_ref, high_ref):
    for tile in range(2):
        for j in range(10):
            if layer < WIDTH:
                low_ref[band, layer, tile * 10 + j] = tiles[tile][j]
            if layer >= 1:
                high_ref[band, layer - 1, tile * 10 + j] = tiles[tile][j]
    for j in range(5):
        both = pair(tiles[2][j], tiles[2][j + 5])
        if layer < WIDTH:
            low_ref[band, layer, 20 + j] = both
        if layer >= 1:
            high_ref[band, layer - 1, 20 + j] = both


def send_edges(tiles, band, layer, edge_ref):
    for side, (start, sublane) in enumerate(((0, 0), (6, 7))):
        for j in range(4):
            for tile in range(2):
                at = j * 10 + layer * 2 + tile
                edge_ref[side, band, at : at + 1, :] = tiles[tile][start + j][sublane : sublane + 1]
        for j in range(2):
            both = pair(tiles[2][start + j], tiles[2][start + j + 2])
            at = 40 + j * 5 + layer
            edge_ref[side, band, at : at + 1, :] = both[sublane : sublane + 1]


def parity(axis):
    return lax.rem(lax.axis_index(axis), 2)


def by_parity(axis, body, first, second):
    @pl.when(parity(axis) == 0)
    def even():
        body(first, second)

    @pl.when(parity(axis) == 1)
    def odd():
        body(second, first)


def hand_edges(edge_ref, inner_ref, outer_ref):
    def copy(low_ref, high_ref):
        for side, ref in enumerate((low_ref, high_ref)):
            for band in range(BANDS):
                ref[band * EDGE_ROWS : (band + 1) * EDGE_ROWS, :] = edge_ref[side, band, 0:EDGE_ROWS, :]
            ref[BANDS * EDGE_ROWS : EDGE[0], :] = jnp.zeros((EDGE[0] - BANDS * EDGE_ROWS, 128), F32)

    by_parity("dy", copy, outer_ref, inner_ref)


def split_kernel(field_ref, state_ref, far_ref, near_ref, inner_ref, outer_ref, stage_ref, edge_ref):
    def body(side_low_ref, side_high_ref):
        def one_band(band, carry):
            for layer in range(LAYERS):
                for tile in range(2):
                    stage_ref[tile] = field_ref[band, layer, :, tile * 128 : tile * 128 + 128]
                stage_ref[2, :, 0:64] = field_ref[band, layer, :, 256:320]
                tiles = [[stage_ref[tile, pl.ds(j, 8, stride=10), :] for j in range(10)] for tile in range(3)]
                for tile in range(3):
                    for j in range(10):
                        state_ref[band, layer, tile, j] = tiles[tile][j]
                send_sides(tiles, band, layer, side_low_ref, side_high_ref)
                send_edges(tiles, band, layer, edge_ref)
            return carry

        lax.fori_loop(0, BANDS, one_band, 0)

    by_parity("dx", body, far_ref, near_ref)
    hand_edges(edge_ref, inner_ref, outer_ref)


def inner_kernel(first, *refs):
    if first:
        state_ref, potential_ref, cutoff_ref, upper_ref, out_ref, diagonal_ref, wide_ref, stage_ref = refs
    else:
        state_ref, previous_ref, diagonal_ref, cutoff_ref, upper_ref, out_ref, wide_ref = refs
    center, per_half_width = bounds(cutoff_ref, upper_ref)
    if first:
        shift = center + 1.5 * stencil_weights[0]
        for layer in range(LAYERS):
            for tile in range(2):
                stage_ref[tile] = potential_ref[layer, :, tile * 128 : tile * 128 + 128]
            stage_ref[2, :, 0:64] = potential_ref[layer, :, 256:320]
            for tile in range(3):
                for j in range(10):
                    cells = stage_ref[tile, pl.ds(j, 8, stride=10), :]
                    diagonal_ref[layer, tile, j] = 2.0 * ((cells - shift) * per_half_width)
    factor = 1.0 if first else 2.0
    weights = [None] + [(-0.5 * factor * stencil_weights[k]) * per_half_width for k in range(1, 5)]
    lane = lanes()
    row = sublanes()

    def plane(at, carry):
        band, layer = at // LAYERS, lax.rem(at, LAYERS)
        for j in range(10):
            tiles = [state_ref[band, layer, tile, j] for tile in range(3)]
            tiles[2] = jnp.where(
                lane < 64, tiles[2], jnp.where(lane < 96, pltpu.roll(tiles[0], 64, 1), pltpu.roll(tiles[2], 64, 1))
            )
            for tile in range(3):
                wide_ref[tile, j] = tiles[tile]
        for tile in range(3):
            ext = [wide_ref[tile, j] for j in range(10)]
            below = [jnp.where(row > 0, pltpu.roll(cells, 1, 0), 0.0) for cells in ext[6:]]
            above = [jnp.where(row < 7, pltpu.roll(cells, 7, 0), 0.0) for cells in ext[:4]]
            ext = below + ext + above
            for j in range(10):
                total = None
                for k in range(1, 5):
                    part = weights[k] * (ext[j + 4 + k] + ext[j + 4 - k])
                    total = part if total is None else total + part
                out_ref[band, layer, tile, j] = total
        for j in range(10):
            mid = [wide_ref[tile, j] for tile in range(3)]
            lefts = [pltpu.roll(cells, 1, 1) for cells in mid]
            lefts = [jnp.where(lane < 1, lefts[(tile + 2) % 3], lefts[tile]) for tile in range(3)]
            rights = [pltpu.roll(cells, 127, 1) for cells in mid]
            rights = [jnp.where(lane < 127, rights[tile], rights[(tile + 1) % 3]) for tile in range(3)]
            ups, downs = [], []
            for tile in range(3):
                centre = weights[3] * mid[tile]
                ups.append(centre + weights[2] * lefts[tile] + weights[4] * rights[tile])
                downs.append(centre + weights[4] * lefts[tile] + weights[2] * rights[tile])
            ups = [pltpu.roll(up, 125, 1) for up in ups]
            downs = [pltpu.roll(down, 3, 1) for down in downs]
            for tile in range(3):
                up = ups[2] if tile == 2 else jnp.where(lane < 125, ups[tile], ups[tile + 1])
                total = up + jnp.where(lane < 3, downs[(tile + 2) % 3], downs[tile])
                total += weights[1] * (lefts[tile] + rights[tile])
                out_ref[band, layer, tile, j] += total
        return carry

    lax.fori_loop(0, BANDS * LAYERS, plane, 0)

    def column(at, carry):
        band, j = at // 10, lax.rem(at, 10)
        for tile in range(3):
            mids = [state_ref[band, layer, tile, j] for layer in range(LAYERS)]
            for layer in range(LAYERS):
                total = out_ref[band, layer, tile, j]
                for k in range(1, 5):
                    near = [mids[at] for at in (layer - k, layer + k) if 0 <= at < LAYERS]
                    if near:
                        total += weights[k] * sum(near[1:], near[0])
                diagonal = diagonal_ref[layer, tile, j] * mids[layer]
                if first:
                    out_ref[band, layer, tile, j] = total + 0.5 * diagonal
                else:
                    out_ref[band, layer, tile, j] = total + (diagonal - previous_ref[band, layer, tile, j])
        return carry

    lax.fori_loop(0, BANDS * 10, column, 0)


def outer_kernel(first, last, *refs):
    part_ref, far_in_ref, near_in_ref, inner_in_ref, outer_in_ref, cutoff_ref, upper_ref, *refs = refs
    if last:
        whole_ref, rim_ref = refs
        state_ref, far_ref, near_ref, edge_ref = None, None, None, None
    else:
        state_ref, far_ref, near_ref, inner_ref, outer_ref, rim_ref, edge_ref = refs
        whole_ref = None
    _, per_half_width = bounds(cutoff_ref, upper_ref)
    factor = 1.0 if first else 2.0
    weights = [None] + [(-0.5 * factor * stencil_weights[k]) * per_half_width for k in range(1, 5)]

    def halos(ref, band):
        start = band * EDGE_ROWS
        whole = [ref[start + j * 10 : start + j * 10 + 10, :] for j in range(4)]
        half = [ref[start + 40 + j * 5 : start + 48 + j * 5, :] for j in range(2)]
        return whole, half + [pltpu.roll(rows, 64, 1) for rows in half]

    def rims(below_ref, above_ref):
        for band in range(BANDS):
            for below, above, rows in zip(halos(below_ref, band), halos(above_ref, band), (slice(0, 10), slice(10, 18))):
                for j in range(4):
                    rim_ref[band, 0, j, rows, :] = sum(weights_of(below[4 + j - k], k) for k in range(j + 1, 5))
                    rim_ref[band, 1, j, rows, :] = sum(weights_of(above[j + k - 4], k) for k in range(4 - j, 5))

    def weights_of(rows, k):
        return (-0.5 * factor * stencil_weights[k]) * rows * per_half_width[0:1]

    by_parity("dy", rims, outer_in_ref, inner_in_ref)

    def body(low, high):
        add_outside(weights, part_ref, rim_ref, low, high, state_ref, edge_ref, whole_ref)

    by_parity("dx", body, (far_in_ref, far_ref), (near_in_ref, near_ref))
    if not last:
        hand_edges(edge_ref, inner_ref, outer_ref)


def add_outside(weights, part_ref, rim_ref, low, high, state_ref, edge_ref, whole_ref):
    low_ref, side_low_ref = low
    high_ref, side_high_ref = high
    last = whole_ref is not None
    row = sublanes()

    def one_band(band, carry):
        for layer in range(LAYERS):
            outside = []
            for v in range(25):
                terms = [weights[layer + 4 - i] * low_ref[band, i, v] for i in range(layer, 4)]
                terms += [weights[5 + i - layer] * high_ref[band, i, v] for i in range(layer)]
                outside.append((terms[0] + terms[1]) + (terms[2] + terms[3]))
            tiles = []
            for tile in range(3):
                cells = []
                for j in range(10):
                    if tile < 2:
                        extra = outside[tile * 10 + j]
                    elif j < 5:
                        extra = outside[20 + j]
                    else:
                        extra = pltpu.roll(outside[15 + j], 64, 1)
                    cell = part_ref[band, layer, tile, j] + extra
                    at = layer * 2 + tile if tile < 2 else 10 + layer
                    if j < 4:
                        cell += jnp.where(row == 0, rim_ref[band, 0, j, at : at + 1, :], 0.0)
                    if j >= 6:
                        cell += jnp.where(row == 7, rim_ref[band, 1, j - 6, at : at + 1, :], 0.0)
                    cells.append(cell)
                tiles.append(cells)
            if last:
                packed = tiles[0] + tiles[1] + [pair(tiles[2][j], tiles[2][j + 5]) for j in range(5)]
                for v in range(25):
                    place = layer * 25 + v
                    whole_ref[place // 32, band, place % 32] = packed[v]
            else:
                for tile in range(3):
                    for j in range(10):
                        state_ref[band, layer, tile, j] = tiles[tile][j]
                send_sides(tiles, band, layer, side_low_ref, side_high_ref)
                send_edges(tiles, band, layer, edge_ref)
        if last:
            for place in range(125, 128):
                whole_ref[place // 32, band, place % 32] = jnp.zeros((8, 128), F32)
        return carry

    lax.fori_loop(0, BANDS, one_band, 0)


PAIRS = [(a, b) for a in range(GROUPS * BANDS) for b in range(a + 1)]


def overlap_kernel(whole_ref, sums_ref, row_ref):
    def accumulate(at, totals):
        cells = [whole_ref[a // BANDS, a % BANDS, at] for a in range(GROUPS * BANDS)]
        return tuple(total + cells[a] * cells[b] for total, (a, b) in zip(totals, PAIRS))

    totals = lax.fori_loop(0, 32, accumulate, tuple(jnp.zeros((8, 128), F32) for _ in PAIRS))
    row_ref[...] = jnp.zeros_like(row_ref)
    for at, total in enumerate(totals):
        row_ref[at : at + 1, :] = jnp.sum(total, axis=0, keepdims=True)
    sums = lax.dot_general(
        jnp.ones((8, 128), F32),
        row_ref[...],
        (((1,), (1,)), ((), ())),
        precision=lax.Precision.HIGHEST,
        preferred_element_type=F32,
    )
    sums_ref[...] = jnp.broadcast_to(sums[0:1].reshape(1, 1, 128), sums_ref.shape)


def rotate_kernel(cell_count, whole_ref, sums_ref, turned_ref):
    count = sums_ref.shape[0] // 8
    parts = [jnp.sum(sums_ref[i * count : (i + 1) * count], axis=0) for i in range(8)]
    while len(parts) > 1:
        parts = [parts[i] + parts[i + 1] for i in range(0, len(parts), 2)]
    row = parts[0] * (1.0 / cell_count)
    extent = GROUPS * BANDS
    matrix = {}
    for at, place in enumerate(PAIRS):
        matrix[place] = jnp.broadcast_to(row[:, at : at + 1], (8, 128))
    factor = {}
    scale = []
    for b in range(extent):
        running = matrix[b, b]
        for s in range(b):
            running = running - factor[b, s] * factor[b, s]
        scale.append(1.0 / jnp.sqrt(running))
        for a in range(b + 1, extent):
            running = matrix[a, b]
            for s in range(b):
                running = running - factor[a, s] * factor[b, s]
            factor[a, b] = running * scale[b]
    inverse = {}
    for target in range(extent):
        inverse[target, target] = scale[target]
        for a in range(target):
            running = factor[target, a] * inverse[a, a]
            for source in range(a + 1, target):
                running = running + factor[target, source] * inverse[source, a]
            inverse[target, a] = -running * scale[target]

    def turn(at, carry):
        cells = [whole_ref[a // BANDS, a % BANDS, at] for a in range(extent)]
        for j in range(extent):
            total = inverse[j, 0] * cells[0]
            for a in range(1, j + 1):
                total = total + inverse[j, a] * cells[a]
            turned_ref[j // BANDS, j % BANDS, at] = total
        return carry

    lax.fori_loop(0, 32, turn, 0)


def merge_kernel(whole_ref, out_ref, stage_ref, plane_ref, sems):
    def copy_out(at):
        return pltpu.make_async_copy(plane_ref.at[at], out_ref.at[at // LAYERS, at % LAYERS], sems.at[at])

    for at in range(BANDS * LAYERS):
        band, layer = at // LAYERS, at % LAYERS
        for v in range(25):
            place = layer * 25 + v
            cell = whole_ref[place // 32, band, place % 32]
            if v < 20:
                stage_ref[v // 10, pl.ds(v % 10, 8, stride=10), :] = cell
            else:
                stage_ref[2, pl.ds(v - 20, 8, stride=10), :] = cell
                stage_ref[2, pl.ds(v - 15, 8, stride=10), :] = pltpu.roll(cell, 64, 1)
        for tile in range(2):
            plane_ref[at, :, tile * 128 : tile * 128 + 128] = stage_ref[tile]
        plane_ref[at, :, 256:320] = stage_ref[2, :, 0:64]
        copy_out(at).start()
    for at in range(BANDS * LAYERS):
        copy_out(at).wait()


def swapped(array, axis, partner):
    return lax.ppermute(array, axis, [(i, partner(i)) for i in range(lax.axis_size(axis))])


def beside(array, axis, offset):
    count = lax.axis_size(axis)
    return swapped(array, axis, lambda i: (i + (offset if i % 2 == 0 else -offset)) % count)


def exchange(whole):
    flat = whole.reshape(GROUPS, BANDS * 32 * 8, 128)
    return lax.all_to_all(flat, "band", 0, 0).reshape(whole.shape)


def local(band_fields, potential, cutoff, upper_bound):
    devices = lax.axis_size("dx") * lax.axis_size("dy") * lax.axis_size("band")
    cell_count = float(LAYERS * 80 * 320 * lax.axis_size("dx") * lax.axis_size("dy"))
    cutoff = cutoff.reshape(1, 1)
    upper_bound = upper_bound.reshape(1, 1)
    stage = (3, 80, 128)
    edges = (2, BANDS, 56, 128)
    state, far, near, inner, outer = call(
        split_kernel, (STATE, SIDE, SIDE, EDGE, EDGE), scratch=(stage, edges)
    )(band_fields)
    previous = diagonal = None
    for step in range(4):
        first, last = step == 0, step == 3
        far = beside(far, "dx", -1)
        near = beside(near, "dx", 1)
        inner = beside(inner, "dy", 1)
        outer = beside(outer, "dy", -1)
        wide = (3, 10, 8, 128)
        if first:
            part, diagonal = call(
                functools.partial(inner_kernel, True), (STATE, STATE[1:]), scratch=(wide, stage)
            )(state, potential, cutoff, upper_bound)
        else:
            (part,) = call(functools.partial(inner_kernel, False), (STATE,), scratch=(wide,))(
                state, previous, diagonal, cutoff, upper_bound
            )
        previous = state
        arguments = (part, far, near, inner, outer, cutoff, upper_bound)
        rim = (BANDS, 2, 4, 24, 128)
        if last:
            (whole,) = call(functools.partial(outer_kernel, first, last), (WHOLE,), scratch=(rim,))(*arguments)
        else:
            state, far, near, inner, outer = call(
                functools.partial(outer_kernel, first, last),
                (STATE, SIDE, SIDE, EDGE, EDGE),
                scratch=(rim, edges),
            )(*arguments)
    whole = exchange(whole)
    (sums,) = call(overlap_kernel, ((devices, 1, 128),), scratch=((128, 128),))(whole)
    sums = lax.all_to_all(sums, ("dy", "band", "dx"), 0, 0)
    (turned,) = call(functools.partial(rotate_kernel, cell_count), (WHOLE,))(whole, sums)
    turned = exchange(turned)
    planes = BANDS * LAYERS
    (rotated,) = call(
        merge_kernel,
        ((BANDS, LAYERS, 80, 320),),
        scratch=(stage, (planes, 80, 320)),
        semaphores=planes,
        out_specs=(pl.BlockSpec(memory_space=pl.ANY),),
    )(turned)
    return rotated


def solution(mesh):
    in_specs = (P("band", "dx", "dy", None), P("dx", "dy", None), P(), P())
    out_specs = P("band", "dx", "dy", None)
    return jax.shard_map(local, mesh=mesh, in_specs=in_specs, out_specs=out_specs, check_vma=False)
```

```python
import functools

import jax
import jax.numpy as jnp
from jax import lax
from jax.experimental import pallas as pl
from jax.experimental.pallas import tpu as pltpu
from jax.sharding import PartitionSpec as P

BANDS = 2
LAYERS = 5
WIDTH = 4
GROUPS = 4
F32 = jnp.float32

stencil_weights = (-205.0 / 72.0, 8.0 / 5.0, -1.0 / 5.0, 8.0 / 315.0, -1.0 / 560.0)

STATE = (BANDS, LAYERS, 3, 10, 8, 128)
SIDE = (BANDS, WIDTH, 25, 8, 128)
EDGE = (104, 128)
EDGE_ROWS = 50
PIECE = (BANDS, 32, 8, 128)


def call(kernel, outs, scratch=(), semaphores=0, **kwargs):
    scratch = [pltpu.VMEM(shape, F32) for shape in scratch]
    if semaphores:
        scratch.append(pltpu.SemaphoreType.DMA((semaphores,)))
    return pl.pallas_call(
        kernel,
        out_shape=tuple(jax.ShapeDtypeStruct(shape, F32) for shape in outs),
        scratch_shapes=scratch,
        compiler_params=pltpu.CompilerParams(vmem_limit_bytes=16 * 1024 * 1024),
        cost_estimate=pl.CostEstimate(flops=4_000_000, bytes_accessed=4_000_000, transcendentals=0),
        **kwargs,
    )


def lanes():
    return lax.broadcasted_iota(jnp.int32, (8, 128), 1)


def sublanes():
    return lax.broadcasted_iota(jnp.int32, (8, 128), 0)


def pair(low, high):
    return jnp.where(lanes() < 64, low, pltpu.roll(high, 64, 1))


def bounds(cutoff_ref, upper_ref):
    low = jnp.broadcast_to(cutoff_ref[...], (8, 128))
    high = jnp.broadcast_to(upper_ref[...], (8, 128))
    return 0.5 * (low + high), 1.0 / (0.5 * (high - low))


def send_sides(tiles, band, layer, low_ref, high_ref):
    for tile in range(2):
        for j in range(10):
            if layer < WIDTH:
                low_ref[band, layer, tile * 10 + j] = tiles[tile][j]
            if layer >= 1:
                high_ref[band, layer - 1, tile * 10 + j] = tiles[tile][j]
    for j in range(5):
        both = pair(tiles[2][j], tiles[2][j + 5])
        if layer < WIDTH:
            low_ref[band, layer, 20 + j] = both
        if layer >= 1:
            high_ref[band, layer - 1, 20 + j] = both


def send_edges(tiles, band, layer, edge_ref):
    for side, (start, sublane) in enumerate(((0, 0), (6, 7))):
        for j in range(4):
            for tile in range(2):
                at = j * 10 + layer * 2 + tile
                edge_ref[side, band, at : at + 1, :] = tiles[tile][start + j][sublane : sublane + 1]
        for j in range(2):
            both = pair(tiles[2][start + j], tiles[2][start + j + 2])
            at = 40 + j * 5 + layer
            edge_ref[side, band, at : at + 1, :] = both[sublane : sublane + 1]


def parity(axis):
    return lax.rem(lax.axis_index(axis), 2)


def by_parity(axis, body, first, second):
    @pl.when(parity(axis) == 0)
    def even():
        body(first, second)

    @pl.when(parity(axis) == 1)
    def odd():
        body(second, first)


def hand_edges(edge_ref, inner_ref, outer_ref):
    def copy(low_ref, high_ref):
        for side, ref in enumerate((low_ref, high_ref)):
            for band in range(BANDS):
                ref[band * EDGE_ROWS : (band + 1) * EDGE_ROWS, :] = edge_ref[side, band, 0:EDGE_ROWS, :]
            ref[BANDS * EDGE_ROWS : EDGE[0], :] = jnp.zeros((EDGE[0] - BANDS * EDGE_ROWS, 128), F32)

    by_parity("dy", copy, outer_ref, inner_ref)


def split_kernel(field_ref, state_ref, far_ref, near_ref, inner_ref, outer_ref, stage_ref, edge_ref):
    def body(side_low_ref, side_high_ref):
        def one_band(band, carry):
            for layer in range(LAYERS):
                for tile in range(2):
                    stage_ref[tile] = field_ref[band, layer, :, tile * 128 : tile * 128 + 128]
                stage_ref[2, :, 0:64] = field_ref[band, layer, :, 256:320]
                tiles = [[stage_ref[tile, pl.ds(j, 8, stride=10), :] for j in range(10)] for tile in range(3)]
                for tile in range(3):
                    for j in range(10):
                        state_ref[band, layer, tile, j] = tiles[tile][j]
                send_sides(tiles, band, layer, side_low_ref, side_high_ref)
                send_edges(tiles, band, layer, edge_ref)
            return carry

        lax.fori_loop(0, BANDS, one_band, 0)

    by_parity("dx", body, far_ref, near_ref)
    hand_edges(edge_ref, inner_ref, outer_ref)


def inner_kernel(first, *refs):
    if first:
        state_ref, potential_ref, cutoff_ref, upper_ref, out_ref, diagonal_ref, wide_ref, stage_ref = refs
    else:
        state_ref, previous_ref, diagonal_ref, cutoff_ref, upper_ref, out_ref, wide_ref = refs
    center, per_half_width = bounds(cutoff_ref, upper_ref)
    if first:
        shift = center + 1.5 * stencil_weights[0]
        for layer in range(LAYERS):
            for tile in range(2):
                stage_ref[tile] = potential_ref[layer, :, tile * 128 : tile * 128 + 128]
            stage_ref[2, :, 0:64] = potential_ref[layer, :, 256:320]
            for tile in range(3):
                for j in range(10):
                    cells = stage_ref[tile, pl.ds(j, 8, stride=10), :]
                    diagonal_ref[layer, tile, j] = 2.0 * ((cells - shift) * per_half_width)
    factor = 1.0 if first else 2.0
    weights = [None] + [(-0.5 * factor * stencil_weights[k]) * per_half_width for k in range(1, 5)]
    lane = lanes()
    row = sublanes()

    def plane(at, carry):
        band, layer = at // LAYERS, lax.rem(at, LAYERS)
        for j in range(10):
            tiles = [state_ref[band, layer, tile, j] for tile in range(3)]
            tiles[2] = jnp.where(
                lane < 64, tiles[2], jnp.where(lane < 96, pltpu.roll(tiles[0], 64, 1), pltpu.roll(tiles[2], 64, 1))
            )
            for tile in range(3):
                wide_ref[tile, j] = tiles[tile]
        for tile in range(3):
            ext = [wide_ref[tile, j] for j in range(10)]
            below = [jnp.where(row > 0, pltpu.roll(cells, 1, 0), 0.0) for cells in ext[6:]]
            above = [jnp.where(row < 7, pltpu.roll(cells, 7, 0), 0.0) for cells in ext[:4]]
            ext = below + ext + above
            for j in range(10):
                total = None
                for k in range(1, 5):
                    part = weights[k] * (ext[j + 4 + k] + ext[j + 4 - k])
                    total = part if total is None else total + part
                out_ref[band, layer, tile, j] = total
        for j in range(10):
            mid = [wide_ref[tile, j] for tile in range(3)]
            lefts = [pltpu.roll(cells, 1, 1) for cells in mid]
            lefts = [jnp.where(lane < 1, lefts[(tile + 2) % 3], lefts[tile]) for tile in range(3)]
            rights = [pltpu.roll(cells, 127, 1) for cells in mid]
            rights = [jnp.where(lane < 127, rights[tile], rights[(tile + 1) % 3]) for tile in range(3)]
            ups, downs = [], []
            for tile in range(3):
                centre = weights[3] * mid[tile]
                ups.append(centre + weights[2] * lefts[tile] + weights[4] * rights[tile])
                downs.append(centre + weights[4] * lefts[tile] + weights[2] * rights[tile])
            ups = [pltpu.roll(up, 125, 1) for up in ups]
            downs = [pltpu.roll(down, 3, 1) for down in downs]
            for tile in range(3):
                up = ups[2] if tile == 2 else jnp.where(lane < 125, ups[tile], ups[tile + 1])
                total = up + jnp.where(lane < 3, downs[(tile + 2) % 3], downs[tile])
                total += weights[1] * (lefts[tile] + rights[tile])
                out_ref[band, layer, tile, j] += total
        return carry

    lax.fori_loop(0, BANDS * LAYERS, plane, 0)

    def column(at, carry):
        band, j = at // 10, lax.rem(at, 10)
        for tile in range(3):
            mids = [state_ref[band, layer, tile, j] for layer in range(LAYERS)]
            for layer in range(LAYERS):
                total = out_ref[band, layer, tile, j]
                for k in range(1, 5):
                    near = [mids[at] for at in (layer - k, layer + k) if 0 <= at < LAYERS]
                    if near:
                        total += weights[k] * sum(near[1:], near[0])
                diagonal = diagonal_ref[layer, tile, j] * mids[layer]
                if first:
                    out_ref[band, layer, tile, j] = total + 0.5 * diagonal
                else:
                    out_ref[band, layer, tile, j] = total + (diagonal - previous_ref[band, layer, tile, j])
        return carry

    lax.fori_loop(0, BANDS * 10, column, 0)


def outer_kernel(first, last, *refs):
    part_ref, far_in_ref, near_in_ref, inner_in_ref, outer_in_ref, cutoff_ref, upper_ref, *refs = refs
    if last:
        *piece_refs, rim_ref, whole_ref = refs
        state_ref, far_ref, near_ref, edge_ref = None, None, None, None
    else:
        state_ref, far_ref, near_ref, inner_ref, outer_ref, rim_ref, edge_ref = refs
        whole_ref = None
    _, per_half_width = bounds(cutoff_ref, upper_ref)
    factor = 1.0 if first else 2.0
    weights = [None] + [(-0.5 * factor * stencil_weights[k]) * per_half_width for k in range(1, 5)]

    def halos(ref, band):
        start = band * EDGE_ROWS
        whole = [ref[start + j * 10 : start + j * 10 + 10, :] for j in range(4)]
        half = [ref[start + 40 + j * 5 : start + 48 + j * 5, :] for j in range(2)]
        return whole, half + [pltpu.roll(rows, 64, 1) for rows in half]

    def rims(below_ref, above_ref):
        for band in range(BANDS):
            for below, above, rows in zip(halos(below_ref, band), halos(above_ref, band), (slice(0, 10), slice(10, 18))):
                for j in range(4):
                    rim_ref[band, 0, j, rows, :] = sum(weights_of(below[4 + j - k], k) for k in range(j + 1, 5))
                    rim_ref[band, 1, j, rows, :] = sum(weights_of(above[j + k - 4], k) for k in range(4 - j, 5))

    def weights_of(rows, k):
        return (-0.5 * factor * stencil_weights[k]) * rows * per_half_width[0:1]

    by_parity("dy", rims, outer_in_ref, inner_in_ref)

    def body(low, high):
        add_outside(weights, part_ref, rim_ref, low, high, state_ref, edge_ref, whole_ref)

    by_parity("dx", body, (far_in_ref, far_ref), (near_in_ref, near_ref))
    if last:
        deal(whole_ref, piece_refs)
    else:
        hand_edges(edge_ref, inner_ref, outer_ref)


def add_outside(weights, part_ref, rim_ref, low, high, state_ref, edge_ref, whole_ref):
    low_ref, side_low_ref = low
    high_ref, side_high_ref = high
    last = whole_ref is not None
    row = sublanes()

    def one_band(band, carry):
        for layer in range(LAYERS):
            outside = []
            for v in range(25):
                terms = [weights[layer + 4 - i] * low_ref[band, i, v] for i in range(layer, 4)]
                terms += [weights[5 + i - layer] * high_ref[band, i, v] for i in range(layer)]
                outside.append((terms[0] + terms[1]) + (terms[2] + terms[3]))
            tiles = []
            for tile in range(3):
                cells = []
                for j in range(10):
                    if tile < 2:
                        extra = outside[tile * 10 + j]
                    elif j < 5:
                        extra = outside[20 + j]
                    else:
                        extra = pltpu.roll(outside[15 + j], 64, 1)
                    cell = part_ref[band, layer, tile, j] + extra
                    at = layer * 2 + tile if tile < 2 else 10 + layer
                    if j < 4:
                        cell += jnp.where(row == 0, rim_ref[band, 0, j, at : at + 1, :], 0.0)
                    if j >= 6:
                        cell += jnp.where(row == 7, rim_ref[band, 1, j - 6, at : at + 1, :], 0.0)
                    cells.append(cell)
                tiles.append(cells)
            if last:
                packed = tiles[0] + tiles[1] + [pair(tiles[2][j], tiles[2][j + 5]) for j in range(5)]
                for v in range(25):
                    place = layer * 25 + v
                    whole_ref[place // 32, band, place % 32] = packed[v]
            else:
                for tile in range(3):
                    for j in range(10):
                        state_ref[band, layer, tile, j] = tiles[tile][j]
                send_sides(tiles, band, layer, side_low_ref, side_high_ref)
                send_edges(tiles, band, layer, edge_ref)
        if last:
            for place in range(125, 128):
                whole_ref[place // 32, band, place % 32] = jnp.zeros((8, 128), F32)
        return carry

    lax.fori_loop(0, BANDS, one_band, 0)


def deal(whole_ref, piece_refs):
    for step, piece_ref in enumerate(piece_refs):
        piece_ref[...] = whole_ref[lax.axis_index("band") ^ step]


def collect(piece_refs, whole_ref):
    for step, piece_ref in enumerate(piece_refs):
        whole_ref[lax.axis_index("band") ^ step] = piece_ref[...]


PAIRS = [(a, b) for a in range(GROUPS * BANDS) for b in range(a + 1)]


def overlap_kernel(*refs):
    *piece_refs, whole_ref, sums_ref, row_ref = refs
    collect(piece_refs, whole_ref)

    def accumulate(at, totals):
        cells = [whole_ref[a // BANDS, a % BANDS, at] for a in range(GROUPS * BANDS)]
        return tuple(total + cells[a] * cells[b] for total, (a, b) in zip(totals, PAIRS))

    totals = lax.fori_loop(0, 32, accumulate, tuple(jnp.zeros((8, 128), F32) for _ in PAIRS))
    row_ref[...] = jnp.zeros_like(row_ref)
    for at, total in enumerate(totals):
        row_ref[at : at + 1, :] = jnp.sum(total, axis=0, keepdims=True)
    sums = lax.dot_general(
        jnp.ones((8, 128), F32),
        row_ref[...],
        (((1,), (1,)), ((), ())),
        precision=lax.Precision.HIGHEST,
        preferred_element_type=F32,
    )
    sums_ref[...] = jnp.broadcast_to(sums[0:1].reshape(1, 1, 128), sums_ref.shape)


def rotate_kernel(cell_count, whole_ref, sums_ref, *refs):
    *piece_refs, turned_ref = refs
    count = sums_ref.shape[0] // 8
    parts = [jnp.sum(sums_ref[i * count : (i + 1) * count], axis=0) for i in range(8)]
    while len(parts) > 1:
        parts = [parts[i] + parts[i + 1] for i in range(0, len(parts), 2)]
    row = parts[0] * (1.0 / cell_count)
    extent = GROUPS * BANDS
    matrix = {}
    for at, place in enumerate(PAIRS):
        matrix[place] = jnp.broadcast_to(row[:, at : at + 1], (8, 128))
    factor = {}
    scale = []
    for b in range(extent):
        running = matrix[b, b]
        for s in range(b):
            running = running - factor[b, s] * factor[b, s]
        scale.append(1.0 / jnp.sqrt(running))
        for a in range(b + 1, extent):
            running = matrix[a, b]
            for s in range(b):
                running = running - factor[a, s] * factor[b, s]
            factor[a, b] = running * scale[b]
    inverse = {}
    for target in range(extent):
        inverse[target, target] = scale[target]
        for a in range(target):
            running = factor[target, a] * inverse[a, a]
            for source in range(a + 1, target):
                running = running + factor[target, source] * inverse[source, a]
            inverse[target, a] = -running * scale[target]

    def turn(at, carry):
        cells = [whole_ref[a // BANDS, a % BANDS, at] for a in range(extent)]
        for j in range(extent):
            total = inverse[j, 0] * cells[0]
            for a in range(1, j + 1):
                total = total + inverse[j, a] * cells[a]
            turned_ref[j // BANDS, j % BANDS, at] = total
        return carry

    lax.fori_loop(0, 32, turn, 0)
    deal(turned_ref, piece_refs)


def merge_kernel(*refs):
    *piece_refs, out_ref, whole_ref, stage_ref, plane_ref, sems = refs
    collect(piece_refs, whole_ref)

    def copy_out(at):
        return pltpu.make_async_copy(plane_ref.at[at], out_ref.at[at // LAYERS, at % LAYERS], sems.at[at])

    for at in range(BANDS * LAYERS):
        band, layer = at // LAYERS, at % LAYERS
        for v in range(25):
            place = layer * 25 + v
            cell = whole_ref[place // 32, band, place % 32]
            if v < 20:
                stage_ref[v // 10, pl.ds(v % 10, 8, stride=10), :] = cell
            else:
                stage_ref[2, pl.ds(v - 20, 8, stride=10), :] = cell
                stage_ref[2, pl.ds(v - 15, 8, stride=10), :] = pltpu.roll(cell, 64, 1)
        for tile in range(2):
            plane_ref[at, :, tile * 128 : tile * 128 + 128] = stage_ref[tile]
        plane_ref[at, :, 256:320] = stage_ref[2, :, 0:64]
        copy_out(at).start()
    for at in range(BANDS * LAYERS):
        copy_out(at).wait()


def swapped(array, axis, partner):
    return lax.ppermute(array, axis, [(i, partner(i)) for i in range(lax.axis_size(axis))])


def beside(array, axis, offset):
    count = lax.axis_size(axis)
    return swapped(array, axis, lambda i: (i + (offset if i % 2 == 0 else -offset)) % count)


def exchange(pieces):
    moved = {step: swapped(pieces[step], "band", lambda i: i ^ step) for step in (2, 1, 3)}
    return [pieces[0], moved[1], moved[2], moved[3]]


def local(band_fields, potential, cutoff, upper_bound):
    devices = lax.axis_size("dx") * lax.axis_size("dy") * lax.axis_size("band")
    cell_count = float(LAYERS * 80 * 320 * lax.axis_size("dx") * lax.axis_size("dy"))
    cutoff = cutoff.reshape(1, 1)
    upper_bound = upper_bound.reshape(1, 1)
    stage = (3, 80, 128)
    edges = (2, BANDS, 56, 128)
    state, far, near, inner, outer = call(
        split_kernel, (STATE, SIDE, SIDE, EDGE, EDGE), scratch=(stage, edges)
    )(band_fields)
    previous = diagonal = None
    for step in range(4):
        first, last = step == 0, step == 3
        far = beside(far, "dx", -1)
        near = beside(near, "dx", 1)
        inner = beside(inner, "dy", 1)
        outer = beside(outer, "dy", -1)
        wide = (3, 10, 8, 128)
        if first:
            part, diagonal = call(
                functools.partial(inner_kernel, True), (STATE, STATE[1:]), scratch=(wide, stage)
            )(state, potential, cutoff, upper_bound)
        else:
            (part,) = call(functools.partial(inner_kernel, False), (STATE,), scratch=(wide,))(
                state, previous, diagonal, cutoff, upper_bound
            )
        previous = state
        arguments = (part, far, near, inner, outer, cutoff, upper_bound)
        rim = (BANDS, 2, 4, 24, 128)
        if last:
            pieces = call(
                functools.partial(outer_kernel, first, last),
                (PIECE,) * 4,
                scratch=(rim, (GROUPS,) + PIECE),
            )(*arguments)
        else:
            state, far, near, inner, outer = call(
                functools.partial(outer_kernel, first, last),
                (STATE, SIDE, SIDE, EDGE, EDGE),
                scratch=(rim, edges),
            )(*arguments)
    pieces = exchange(pieces)
    whole, sums = call(overlap_kernel, ((GROUPS,) + PIECE, (devices, 1, 128)), scratch=((128, 128),))(*pieces)
    sums = lax.all_to_all(sums, ("dy", "band", "dx"), 0, 0)
    pieces = call(
        functools.partial(rotate_kernel, cell_count), (PIECE,) * 4, scratch=((GROUPS,) + PIECE,)
    )(whole, sums)
    pieces = exchange(pieces)
    planes = BANDS * LAYERS
    (rotated,) = call(
        merge_kernel,
        ((BANDS, LAYERS, 80, 320),),
        scratch=((GROUPS,) + PIECE, stage, (planes, 80, 320)),
        semaphores=planes,
        out_specs=(pl.BlockSpec(memory_space=pl.ANY),),
    )(*pieces)
    return rotated


def solution(mesh):
    in_specs = (P("band", "dx", "dy", None), P("dx", "dy", None), P(), P())
    out_specs = P("band", "dx", "dy", None)
    return jax.shard_map(local, mesh=mesh, in_specs=in_specs, out_specs=out_specs, check_vma=False)
```

```python
import functools

import jax
import jax.numpy as jnp
from jax import lax
from jax.experimental import pallas as pl
from jax.experimental.pallas import tpu as pltpu
from jax.sharding import PartitionSpec as P

BANDS = 2
LAYERS = 5
WIDTH = 4
GROUPS = 4
F32 = jnp.float32

stencil_weights = (-205.0 / 72.0, 8.0 / 5.0, -1.0 / 5.0, 8.0 / 315.0, -1.0 / 560.0)

STATE = (BANDS, LAYERS, 3, 10, 8, 128)
SIDE = (BANDS, WIDTH, 25, 8, 128)
EDGE = (104, 128)
EDGE_ROWS = 50
PIECE = (BANDS, 32, 8, 128)


def call(kernel, outs, scratch=(), semaphores=0, **kwargs):
    scratch = [pltpu.VMEM(shape, F32) for shape in scratch]
    if semaphores:
        scratch.append(pltpu.SemaphoreType.DMA((semaphores,)))
    return pl.pallas_call(
        kernel,
        out_shape=tuple(jax.ShapeDtypeStruct(shape, F32) for shape in outs),
        scratch_shapes=scratch,
        compiler_params=pltpu.CompilerParams(vmem_limit_bytes=16 * 1024 * 1024),
        cost_estimate=pl.CostEstimate(flops=4_000_000, bytes_accessed=4_000_000, transcendentals=0),
        **kwargs,
    )


def lanes():
    return lax.broadcasted_iota(jnp.int32, (8, 128), 1)


def sublanes():
    return lax.broadcasted_iota(jnp.int32, (8, 128), 0)


def pair(low, high):
    return jnp.where(lanes() < 64, low, pltpu.roll(high, 64, 1))


def bounds(cutoff_ref, upper_ref):
    low = jnp.broadcast_to(cutoff_ref[...], (8, 128))
    high = jnp.broadcast_to(upper_ref[...], (8, 128))
    return 0.5 * (low + high), 1.0 / (0.5 * (high - low))


def send_sides(tiles, band, layer, low_ref, high_ref):
    for tile in range(2):
        for j in range(10):
            if layer < WIDTH:
                low_ref[band, layer, tile * 10 + j] = tiles[tile][j]
            if layer >= 1:
                high_ref[band, layer - 1, tile * 10 + j] = tiles[tile][j]
    for j in range(5):
        both = pair(tiles[2][j], tiles[2][j + 5])
        if layer < WIDTH:
            low_ref[band, layer, 20 + j] = both
        if layer >= 1:
            high_ref[band, layer - 1, 20 + j] = both


def send_edges(tiles, band, layer, edge_ref):
    for side, (start, sublane) in enumerate(((0, 0), (6, 7))):
        for j in range(4):
            for tile in range(2):
                at = j * 10 + layer * 2 + tile
                edge_ref[side, band, at : at + 1, :] = tiles[tile][start + j][sublane : sublane + 1]
        for j in range(2):
            both = pair(tiles[2][start + j], tiles[2][start + j + 2])
            at = 40 + j * 5 + layer
            edge_ref[side, band, at : at + 1, :] = both[sublane : sublane + 1]


def parity(axis):
    return lax.rem(lax.axis_index(axis), 2)


def by_parity(axis, body, first, second):
    @pl.when(parity(axis) == 0)
    def even():
        body(first, second)

    @pl.when(parity(axis) == 1)
    def odd():
        body(second, first)


def hand_edges(edge_ref, inner_ref, outer_ref):
    def copy(low_ref, high_ref):
        for side, ref in enumerate((low_ref, high_ref)):
            for band in range(BANDS):
                ref[band * EDGE_ROWS : (band + 1) * EDGE_ROWS, :] = edge_ref[side, band, 0:EDGE_ROWS, :]
            ref[BANDS * EDGE_ROWS : EDGE[0], :] = jnp.zeros((EDGE[0] - BANDS * EDGE_ROWS, 128), F32)

    by_parity("dy", copy, outer_ref, inner_ref)


def split_kernel(field_ref, state_ref, far_ref, near_ref, inner_ref, outer_ref, stage_ref, edge_ref):
    def body(side_low_ref, side_high_ref):
        def one_band(band, carry):
            for layer in range(LAYERS):
                for tile in range(2):
                    stage_ref[tile] = field_ref[band, layer, :, tile * 128 : tile * 128 + 128]
                stage_ref[2, :, 0:64] = field_ref[band, layer, :, 256:320]
                tiles = [[stage_ref[tile, pl.ds(j, 8, stride=10), :] for j in range(10)] for tile in range(3)]
                for tile in range(3):
                    for j in range(10):
                        state_ref[band, layer, tile, j] = tiles[tile][j]
                send_sides(tiles, band, layer, side_low_ref, side_high_ref)
                send_edges(tiles, band, layer, edge_ref)
            return carry

        lax.fori_loop(0, BANDS, one_band, 0)

    by_parity("dx", body, far_ref, near_ref)
    hand_edges(edge_ref, inner_ref, outer_ref)


def inner_kernel(first, *refs):
    if first:
        state_ref, potential_ref, cutoff_ref, upper_ref, out_ref, diagonal_ref, wide_ref, stage_ref = refs
    else:
        state_ref, previous_ref, diagonal_ref, cutoff_ref, upper_ref, out_ref, wide_ref = refs
    center, per_half_width = bounds(cutoff_ref, upper_ref)
    if first:
        shift = center + 1.5 * stencil_weights[0]
        for layer in range(LAYERS):
            for tile in range(2):
                stage_ref[tile] = potential_ref[layer, :, tile * 128 : tile * 128 + 128]
            stage_ref[2, :, 0:64] = potential_ref[layer, :, 256:320]
            for tile in range(3):
                for j in range(10):
                    cells = stage_ref[tile, pl.ds(j, 8, stride=10), :]
                    diagonal_ref[layer, tile, j] = 2.0 * ((cells - shift) * per_half_width)
    factor = 1.0 if first else 2.0
    weights = [None] + [(-0.5 * factor * stencil_weights[k]) * per_half_width for k in range(1, 5)]
    lane = lanes()
    row = sublanes()

    def plane(at, carry):
        band, layer = at // LAYERS, lax.rem(at, LAYERS)
        for j in range(10):
            tiles = [state_ref[band, layer, tile, j] for tile in range(3)]
            tiles[2] = jnp.where(
                lane < 64, tiles[2], jnp.where(lane < 96, pltpu.roll(tiles[0], 64, 1), pltpu.roll(tiles[2], 64, 1))
            )
            for tile in range(3):
                wide_ref[tile, j] = tiles[tile]
        for tile in range(3):
            ext = [wide_ref[tile, j] for j in range(10)]
            below = [jnp.where(row > 0, pltpu.roll(cells, 1, 0), 0.0) for cells in ext[6:]]
            above = [jnp.where(row < 7, pltpu.roll(cells, 7, 0), 0.0) for cells in ext[:4]]
            ext = below + ext + above
            for j in range(10):
                total = None
                for k in range(1, 5):
                    part = weights[k] * (ext[j + 4 + k] + ext[j + 4 - k])
                    total = part if total is None else total + part
                out_ref[band, layer, tile, j] = total
        for j in range(10):
            mid = [wide_ref[tile, j] for tile in range(3)]
            lefts = [pltpu.roll(cells, 1, 1) for cells in mid]
            lefts = [jnp.where(lane < 1, lefts[(tile + 2) % 3], lefts[tile]) for tile in range(3)]
            rights = [pltpu.roll(cells, 127, 1) for cells in mid]
            rights = [jnp.where(lane < 127, rights[tile], rights[(tile + 1) % 3]) for tile in range(3)]
            ups, downs = [], []
            for tile in range(3):
                centre = weights[3] * mid[tile]
                ups.append(centre + weights[2] * lefts[tile] + weights[4] * rights[tile])
                downs.append(centre + weights[4] * lefts[tile] + weights[2] * rights[tile])
            ups = [pltpu.roll(up, 125, 1) for up in ups]
            downs = [pltpu.roll(down, 3, 1) for down in downs]
            for tile in range(3):
                up = ups[2] if tile == 2 else jnp.where(lane < 125, ups[tile], ups[tile + 1])
                total = up + jnp.where(lane < 3, downs[(tile + 2) % 3], downs[tile])
                total += weights[1] * (lefts[tile] + rights[tile])
                out_ref[band, layer, tile, j] += total
        return carry

    lax.fori_loop(0, BANDS * LAYERS, plane, 0)

    def column(at, carry):
        band, j = at // 10, lax.rem(at, 10)
        for tile in range(3):
            mids = [state_ref[band, layer, tile, j] for layer in range(LAYERS)]
            for layer in range(LAYERS):
                total = out_ref[band, layer, tile, j]
                for k in range(1, 5):
                    near = [mids[at] for at in (layer - k, layer + k) if 0 <= at < LAYERS]
                    if near:
                        total += weights[k] * sum(near[1:], near[0])
                diagonal = diagonal_ref[layer, tile, j] * mids[layer]
                if first:
                    out_ref[band, layer, tile, j] = total + 0.5 * diagonal
                else:
                    out_ref[band, layer, tile, j] = total + (diagonal - previous_ref[band, layer, tile, j])
        return carry

    lax.fori_loop(0, BANDS * 10, column, 0)


def outer_kernel(first, last, *refs):
    part_ref, far_in_ref, near_in_ref, inner_in_ref, outer_in_ref, cutoff_ref, upper_ref, *refs = refs
    if last:
        *piece_refs, rim_ref, whole_ref = refs
        state_ref, far_ref, near_ref, edge_ref = None, None, None, None
    else:
        state_ref, far_ref, near_ref, inner_ref, outer_ref, rim_ref, edge_ref = refs
        whole_ref = None
    _, per_half_width = bounds(cutoff_ref, upper_ref)
    factor = 1.0 if first else 2.0
    weights = [None] + [(-0.5 * factor * stencil_weights[k]) * per_half_width for k in range(1, 5)]

    def halos(ref, band):
        start = band * EDGE_ROWS
        whole = [ref[start + j * 10 : start + j * 10 + 10, :] for j in range(4)]
        half = [ref[start + 40 + j * 5 : start + 48 + j * 5, :] for j in range(2)]
        return whole, half + [pltpu.roll(rows, 64, 1) for rows in half]

    def rims(below_ref, above_ref):
        for band in range(BANDS):
            for below, above, rows in zip(halos(below_ref, band), halos(above_ref, band), (slice(0, 10), slice(10, 18))):
                for j in range(4):
                    rim_ref[band, 0, j, rows, :] = sum(weights_of(below[4 + j - k], k) for k in range(j + 1, 5))
                    rim_ref[band, 1, j, rows, :] = sum(weights_of(above[j + k - 4], k) for k in range(4 - j, 5))

    def weights_of(rows, k):
        return (-0.5 * factor * stencil_weights[k]) * rows * per_half_width[0:1]

    by_parity("dy", rims, outer_in_ref, inner_in_ref)

    def body(low, high):
        add_outside(weights, part_ref, rim_ref, low, high, state_ref, edge_ref, whole_ref)

    by_parity("dx", body, (far_in_ref, far_ref), (near_in_ref, near_ref))
    if last:
        deal(whole_ref, piece_refs)
    else:
        hand_edges(edge_ref, inner_ref, outer_ref)


def add_outside(weights, part_ref, rim_ref, low, high, state_ref, edge_ref, whole_ref):
    low_ref, side_low_ref = low
    high_ref, side_high_ref = high
    last = whole_ref is not None
    row = sublanes()

    def one_band(band, carry):
        for layer in range(LAYERS):
            outside = []
            for v in range(25):
                terms = [weights[layer + 4 - i] * low_ref[band, i, v] for i in range(layer, 4)]
                terms += [weights[5 + i - layer] * high_ref[band, i, v] for i in range(layer)]
                outside.append((terms[0] + terms[1]) + (terms[2] + terms[3]))
            tiles = []
            for tile in range(3):
                cells = []
                for j in range(10):
                    if tile < 2:
                        extra = outside[tile * 10 + j]
                    elif j < 5:
                        extra = outside[20 + j]
                    else:
                        extra = pltpu.roll(outside[15 + j], 64, 1)
                    cell = part_ref[band, layer, tile, j] + extra
                    at = layer * 2 + tile if tile < 2 else 10 + layer
                    if j < 4:
                        cell += jnp.where(row == 0, rim_ref[band, 0, j, at : at + 1, :], 0.0)
                    if j >= 6:
                        cell += jnp.where(row == 7, rim_ref[band, 1, j - 6, at : at + 1, :], 0.0)
                    cells.append(cell)
                tiles.append(cells)
            if last:
                packed = tiles[0] + tiles[1] + [pair(tiles[2][j], tiles[2][j + 5]) for j in range(5)]
                for v in range(25):
                    place = layer * 25 + v
                    whole_ref[place // 32, band, place % 32] = packed[v]
            else:
                for tile in range(3):
                    for j in range(10):
                        state_ref[band, layer, tile, j] = tiles[tile][j]
                send_sides(tiles, band, layer, side_low_ref, side_high_ref)
                send_edges(tiles, band, layer, edge_ref)
        if last:
            for place in range(125, 128):
                whole_ref[place // 32, band, place % 32] = jnp.zeros((8, 128), F32)
        return carry

    lax.fori_loop(0, BANDS, one_band, 0)


def deal(whole_ref, piece_refs):
    for step, piece_ref in enumerate(piece_refs):
        piece_ref[...] = whole_ref[lax.axis_index("band") ^ step]


def collect(piece_refs, whole_ref):
    for step, piece_ref in enumerate(piece_refs):
        whole_ref[lax.axis_index("band") ^ step] = piece_ref[...]


PAIRS = [(a, b) for a in range(GROUPS * BANDS) for b in range(a + 1)]


def overlap_kernel(*refs):
    *piece_refs, whole_ref, sums_ref, row_ref = refs
    collect(piece_refs, whole_ref)

    def accumulate(quad, totals):
        for part in range(4):
            cells = [whole_ref[a // BANDS, a % BANDS, quad * 4 + part] for a in range(GROUPS * BANDS)]
            totals = tuple(total + cells[a] * cells[b] for total, (a, b) in zip(totals, PAIRS))
        return totals

    totals = lax.fori_loop(0, 8, accumulate, tuple(jnp.zeros((8, 128), F32) for _ in PAIRS))
    row_ref[...] = jnp.zeros_like(row_ref)
    for at, total in enumerate(totals):
        row_ref[at : at + 1, :] = jnp.sum(total, axis=0, keepdims=True)
    sums = lax.dot_general(
        jnp.ones((8, 128), F32),
        row_ref[...],
        (((1,), (1,)), ((), ())),
        precision=lax.Precision.HIGHEST,
        preferred_element_type=F32,
    )
    sums_ref[...] = jnp.broadcast_to(sums[0:1].reshape(1, 1, 128), sums_ref.shape)


def rotate_kernel(cell_count, whole_ref, sums_ref, *refs):
    *piece_refs, turned_ref = refs
    count = sums_ref.shape[0] // 8
    parts = [jnp.sum(sums_ref[i * count : (i + 1) * count], axis=0) for i in range(8)]
    while len(parts) > 1:
        parts = [parts[i] + parts[i + 1] for i in range(0, len(parts), 2)]
    row = parts[0] * (1.0 / cell_count)
    extent = GROUPS * BANDS
    matrix = {}
    for at, place in enumerate(PAIRS):
        matrix[place] = jnp.broadcast_to(row[:, at : at + 1], (8, 128))
    factor = {}
    scale = []
    for b in range(extent):
        running = matrix[b, b]
        for s in range(b):
            running = running - factor[b, s] * factor[b, s]
        scale.append(1.0 / jnp.sqrt(running))
        for a in range(b + 1, extent):
            running = matrix[a, b]
            for s in range(b):
                running = running - factor[a, s] * factor[b, s]
            factor[a, b] = running * scale[b]
    inverse = {}
    for target in range(extent):
        inverse[target, target] = scale[target]
        for a in range(target):
            running = factor[target, a] * inverse[a, a]
            for source in range(a + 1, target):
                running = running + factor[target, source] * inverse[source, a]
            inverse[target, a] = -running * scale[target]

    def turn(quad, carry):
        for part in range(4):
            at = quad * 4 + part
            cells = [whole_ref[a // BANDS, a % BANDS, at] for a in range(extent)]
            for j in range(extent):
                total = inverse[j, 0] * cells[0]
                for a in range(1, j + 1):
                    total = total + inverse[j, a] * cells[a]
                turned_ref[j // BANDS, j % BANDS, at] = total
        return carry

    lax.fori_loop(0, 8, turn, 0)
    deal(turned_ref, piece_refs)


def merge_kernel(*refs):
    *piece_refs, out_ref, whole_ref, stage_ref, plane_ref, sems = refs
    collect(piece_refs, whole_ref)

    def copy_out(at):
        return pltpu.make_async_copy(plane_ref.at[at], out_ref.at[at // LAYERS, at % LAYERS], sems.at[at])

    for at in range(BANDS * LAYERS):
        band, layer = at // LAYERS, at % LAYERS
        for v in range(25):
            place = layer * 25 + v
            cell = whole_ref[place // 32, band, place % 32]
            if v < 20:
                stage_ref[v // 10, pl.ds(v % 10, 8, stride=10), :] = cell
            else:
                stage_ref[2, pl.ds(v - 20, 8, stride=10), :] = cell
                stage_ref[2, pl.ds(v - 15, 8, stride=10), :] = pltpu.roll(cell, 64, 1)
        for tile in range(2):
            plane_ref[at, :, tile * 128 : tile * 128 + 128] = stage_ref[tile]
        plane_ref[at, :, 256:320] = stage_ref[2, :, 0:64]
        copy_out(at).start()
    for at in range(BANDS * LAYERS):
        copy_out(at).wait()


def swapped(array, axis, partner):
    return lax.ppermute(array, axis, [(i, partner(i)) for i in range(lax.axis_size(axis))])


def beside(array, axis, offset):
    count = lax.axis_size(axis)
    return swapped(array, axis, lambda i: (i + (offset if i % 2 == 0 else -offset)) % count)


def exchange(pieces):
    moved = {step: swapped(pieces[step], "band", lambda i: i ^ step) for step in (2, 1, 3)}
    return [pieces[0], moved[1], moved[2], moved[3]]


def local(band_fields, potential, cutoff, upper_bound):
    devices = lax.axis_size("dx") * lax.axis_size("dy") * lax.axis_size("band")
    cell_count = float(LAYERS * 80 * 320 * lax.axis_size("dx") * lax.axis_size("dy"))
    cutoff = cutoff.reshape(1, 1)
    upper_bound = upper_bound.reshape(1, 1)
    stage = (3, 80, 128)
    edges = (2, BANDS, 56, 128)
    state, far, near, inner, outer = call(
        split_kernel, (STATE, SIDE, SIDE, EDGE, EDGE), scratch=(stage, edges)
    )(band_fields)
    previous = diagonal = None
    for step in range(4):
        first, last = step == 0, step == 3
        far = beside(far, "dx", -1)
        near = beside(near, "dx", 1)
        inner = beside(inner, "dy", 1)
        outer = beside(outer, "dy", -1)
        wide = (3, 10, 8, 128)
        if first:
            part, diagonal = call(
                functools.partial(inner_kernel, True), (STATE, STATE[1:]), scratch=(wide, stage)
            )(state, potential, cutoff, upper_bound)
        else:
            (part,) = call(functools.partial(inner_kernel, False), (STATE,), scratch=(wide,))(
                state, previous, diagonal, cutoff, upper_bound
            )
        previous = state
        arguments = (part, far, near, inner, outer, cutoff, upper_bound)
        rim = (BANDS, 2, 4, 24, 128)
        if last:
            pieces = call(
                functools.partial(outer_kernel, first, last),
                (PIECE,) * 4,
                scratch=(rim, (GROUPS,) + PIECE),
            )(*arguments)
        else:
            state, far, near, inner, outer = call(
                functools.partial(outer_kernel, first, last),
                (STATE, SIDE, SIDE, EDGE, EDGE),
                scratch=(rim, edges),
            )(*arguments)
    pieces = exchange(pieces)
    whole, sums = call(overlap_kernel, ((GROUPS,) + PIECE, (devices, 1, 128)), scratch=((128, 128),))(*pieces)
    sums = lax.all_to_all(sums, ("dy", "band", "dx"), 0, 0)
    pieces = call(
        functools.partial(rotate_kernel, cell_count), (PIECE,) * 4, scratch=((GROUPS,) + PIECE,)
    )(whole, sums)
    pieces = exchange(pieces)
    planes = BANDS * LAYERS
    (rotated,) = call(
        merge_kernel,
        ((BANDS, LAYERS, 80, 320),),
        scratch=((GROUPS,) + PIECE, stage, (planes, 80, 320)),
        semaphores=planes,
        out_specs=(pl.BlockSpec(memory_space=pl.ANY),),
    )(*pieces)
    return rotated


def solution(mesh):
    in_specs = (P("band", "dx", "dy", None), P("dx", "dy", None), P(), P())
    out_specs = P("band", "dx", "dy", None)
    return jax.shard_map(local, mesh=mesh, in_specs=in_specs, out_specs=out_specs, check_vma=False)
```

```python
import functools

import jax
import jax.numpy as jnp
from jax import lax
from jax.experimental import pallas as pl
from jax.experimental.pallas import tpu as pltpu
from jax.sharding import PartitionSpec as P

BANDS = 2
LAYERS = 5
WIDTH = 4
GROUPS = 4
F32 = jnp.float32

stencil_weights = (-205.0 / 72.0, 8.0 / 5.0, -1.0 / 5.0, 8.0 / 315.0, -1.0 / 560.0)

STATE = (BANDS, LAYERS, 3, 10, 8, 128)
SIDE = (BANDS, WIDTH, 25, 8, 128)
EDGE = (104, 128)
EDGE_ROWS = 50
PIECE = (BANDS, 32, 8, 128)


def call(kernel, outs, scratch=(), semaphores=0, **kwargs):
    scratch = [pltpu.VMEM(shape, F32) for shape in scratch]
    if semaphores:
        scratch.append(pltpu.SemaphoreType.DMA((semaphores,)))
    return pl.pallas_call(
        kernel,
        out_shape=tuple(jax.ShapeDtypeStruct(shape, F32) for shape in outs),
        scratch_shapes=scratch,
        compiler_params=pltpu.CompilerParams(vmem_limit_bytes=16 * 1024 * 1024),
        cost_estimate=pl.CostEstimate(flops=4_000_000, bytes_accessed=4_000_000, transcendentals=0),
        **kwargs,
    )


def lanes():
    return lax.broadcasted_iota(jnp.int32, (8, 128), 1)


def sublanes():
    return lax.broadcasted_iota(jnp.int32, (8, 128), 0)


def pair(low, high):
    return jnp.where(lanes() < 64, low, pltpu.roll(high, 64, 1))


def bounds(cutoff_ref, upper_ref):
    low = jnp.broadcast_to(cutoff_ref[...], (8, 128))
    high = jnp.broadcast_to(upper_ref[...], (8, 128))
    return 0.5 * (low + high), 1.0 / (0.5 * (high - low))


def send_sides(tiles, band, layer, low_ref, high_ref):
    for tile in range(2):
        for j in range(10):
            if layer < WIDTH:
                low_ref[band, layer, tile * 10 + j] = tiles[tile][j]
            if layer >= 1:
                high_ref[band, layer - 1, tile * 10 + j] = tiles[tile][j]
    for j in range(5):
        both = pair(tiles[2][j], tiles[2][j + 5])
        if layer < WIDTH:
            low_ref[band, layer, 20 + j] = both
        if layer >= 1:
            high_ref[band, layer - 1, 20 + j] = both


def send_edges(tiles, band, layer, edge_ref):
    for side, (start, sublane) in enumerate(((0, 0), (6, 7))):
        for j in range(4):
            for tile in range(2):
                at = j * 10 + layer * 2 + tile
                edge_ref[side, band, at : at + 1, :] = tiles[tile][start + j][sublane : sublane + 1]
        for j in range(2):
            both = pair(tiles[2][start + j], tiles[2][start + j + 2])
            at = 40 + j * 5 + layer
            edge_ref[side, band, at : at + 1, :] = both[sublane : sublane + 1]


def parity(axis):
    return lax.rem(lax.axis_index(axis), 2)


def by_parity(axis, body, first, second):
    @pl.when(parity(axis) == 0)
    def even():
        body(first, second)

    @pl.when(parity(axis) == 1)
    def odd():
        body(second, first)


def hand_edges(edge_ref, inner_ref, outer_ref):
    def copy(low_ref, high_ref):
        for side, ref in enumerate((low_ref, high_ref)):
            for band in range(BANDS):
                ref[band * EDGE_ROWS : (band + 1) * EDGE_ROWS, :] = edge_ref[side, band, 0:EDGE_ROWS, :]
            ref[BANDS * EDGE_ROWS : EDGE[0], :] = jnp.zeros((EDGE[0] - BANDS * EDGE_ROWS, 128), F32)

    by_parity("dy", copy, outer_ref, inner_ref)


def split_kernel(field_ref, state_ref, far_ref, near_ref, inner_ref, outer_ref, stage_ref, edge_ref):
    def body(side_low_ref, side_high_ref):
        def one_band(band, carry):
            for layer in range(LAYERS):
                for tile in range(2):
                    stage_ref[tile] = field_ref[band, layer, :, tile * 128 : tile * 128 + 128]
                stage_ref[2, :, 0:64] = field_ref[band, layer, :, 256:320]
                tiles = [[stage_ref[tile, pl.ds(j, 8, stride=10), :] for j in range(10)] for tile in range(3)]
                for tile in range(3):
                    for j in range(10):
                        state_ref[band, layer, tile, j] = tiles[tile][j]
                send_sides(tiles, band, layer, side_low_ref, side_high_ref)
                send_edges(tiles, band, layer, edge_ref)
            return carry

        lax.fori_loop(0, BANDS, one_band, 0)

    by_parity("dx", body, far_ref, near_ref)
    hand_edges(edge_ref, inner_ref, outer_ref)


def inner_kernel(first, *refs):
    if first:
        state_ref, potential_ref, cutoff_ref, upper_ref, out_ref, diagonal_ref, wide_ref, stage_ref = refs
    else:
        state_ref, previous_ref, diagonal_ref, cutoff_ref, upper_ref, out_ref, wide_ref = refs
    center, per_half_width = bounds(cutoff_ref, upper_ref)
    if first:
        shift = center + 1.5 * stencil_weights[0]
        for layer in range(LAYERS):
            for tile in range(2):
                stage_ref[tile] = potential_ref[layer, :, tile * 128 : tile * 128 + 128]
            stage_ref[2, :, 0:64] = potential_ref[layer, :, 256:320]
            for tile in range(3):
                for j in range(10):
                    cells = stage_ref[tile, pl.ds(j, 8, stride=10), :]
                    diagonal_ref[layer, tile, j] = 2.0 * ((cells - shift) * per_half_width)
    factor = 1.0 if first else 2.0
    weights = [None] + [(-0.5 * factor * stencil_weights[k]) * per_half_width for k in range(1, 5)]
    lane = lanes()
    row = sublanes()

    def plane(at, carry):
        band, layer = at // LAYERS, lax.rem(at, LAYERS)
        for j in range(10):
            tiles = [state_ref[band, layer, tile, j] for tile in range(3)]
            tiles[2] = jnp.where(
                lane < 64, tiles[2], jnp.where(lane < 96, pltpu.roll(tiles[0], 64, 1), pltpu.roll(tiles[2], 64, 1))
            )
            for tile in range(3):
                wide_ref[tile, j] = tiles[tile]
        for tile in range(3):
            ext = [wide_ref[tile, j] for j in range(10)]
            below = [jnp.where(row > 0, pltpu.roll(cells, 1, 0), 0.0) for cells in ext[6:]]
            above = [jnp.where(row < 7, pltpu.roll(cells, 7, 0), 0.0) for cells in ext[:4]]
            ext = below + ext + above
            for j in range(10):
                total = None
                for k in range(1, 5):
                    part = weights[k] * (ext[j + 4 + k] + ext[j + 4 - k])
                    total = part if total is None else total + part
                out_ref[band, layer, tile, j] = total
        for j in range(10):
            mid = [wide_ref[tile, j] for tile in range(3)]
            lefts = [pltpu.roll(cells, 1, 1) for cells in mid]
            lefts = [jnp.where(lane < 1, lefts[(tile + 2) % 3], lefts[tile]) for tile in range(3)]
            rights = [pltpu.roll(cells, 127, 1) for cells in mid]
            rights = [jnp.where(lane < 127, rights[tile], rights[(tile + 1) % 3]) for tile in range(3)]
            ups, downs = [], []
            for tile in range(3):
                centre = weights[3] * mid[tile]
                ups.append(centre + weights[2] * lefts[tile] + weights[4] * rights[tile])
                downs.append(centre + weights[4] * lefts[tile] + weights[2] * rights[tile])
            ups = [pltpu.roll(up, 125, 1) for up in ups]
            downs = [pltpu.roll(down, 3, 1) for down in downs]
            for tile in range(3):
                up = ups[2] if tile == 2 else jnp.where(lane < 125, ups[tile], ups[tile + 1])
                total = up + jnp.where(lane < 3, downs[(tile + 2) % 3], downs[tile])
                total += weights[1] * (lefts[tile] + rights[tile])
                out_ref[band, layer, tile, j] += total
        return carry

    lax.fori_loop(0, BANDS * LAYERS, plane, 0)

    def column(at, carry):
        band, j = at // 10, lax.rem(at, 10)
        for tile in range(3):
            mids = [state_ref[band, layer, tile, j] for layer in range(LAYERS)]
            for layer in range(LAYERS):
                total = out_ref[band, layer, tile, j]
                for k in range(1, 5):
                    near = [mids[at] for at in (layer - k, layer + k) if 0 <= at < LAYERS]
                    if near:
                        total += weights[k] * sum(near[1:], near[0])
                diagonal = diagonal_ref[layer, tile, j] * mids[layer]
                if first:
                    out_ref[band, layer, tile, j] = total + 0.5 * diagonal
                else:
                    out_ref[band, layer, tile, j] = total + (diagonal - previous_ref[band, layer, tile, j])
        return carry

    lax.fori_loop(0, BANDS * 10, column, 0)


def outer_kernel(first, last, *refs):
    part_ref, far_in_ref, near_in_ref, inner_in_ref, outer_in_ref, cutoff_ref, upper_ref, *refs = refs
    if last:
        *piece_refs, rim_ref, whole_ref = refs
        state_ref, far_ref, near_ref, edge_ref = None, None, None, None
    else:
        state_ref, far_ref, near_ref, inner_ref, outer_ref, rim_ref, edge_ref = refs
        whole_ref = None
    _, per_half_width = bounds(cutoff_ref, upper_ref)
    factor = 1.0 if first else 2.0
    weights = [None] + [(-0.5 * factor * stencil_weights[k]) * per_half_width for k in range(1, 5)]

    def halos(ref, band):
        start = band * EDGE_ROWS
        whole = [ref[start + j * 10 : start + j * 10 + 10, :] for j in range(4)]
        half = [ref[start + 40 + j * 5 : start + 48 + j * 5, :] for j in range(2)]
        return whole, half + [pltpu.roll(rows, 64, 1) for rows in half]

    def rims(below_ref, above_ref):
        for band in range(BANDS):
            for below, above, rows in zip(halos(below_ref, band), halos(above_ref, band), (slice(0, 10), slice(10, 18))):
                for j in range(4):
                    rim_ref[band, 0, j, rows, :] = sum(weights_of(below[4 + j - k], k) for k in range(j + 1, 5))
                    rim_ref[band, 1, j, rows, :] = sum(weights_of(above[j + k - 4], k) for k in range(4 - j, 5))

    def weights_of(rows, k):
        return (-0.5 * factor * stencil_weights[k]) * rows * per_half_width[0:1]

    by_parity("dy", rims, outer_in_ref, inner_in_ref)

    def body(low, high):
        add_outside(weights, part_ref, rim_ref, low, high, state_ref, edge_ref, whole_ref)

    by_parity("dx", body, (far_in_ref, far_ref), (near_in_ref, near_ref))
    if last:
        deal(whole_ref, piece_refs)
    else:
        hand_edges(edge_ref, inner_ref, outer_ref)


def add_outside(weights, part_ref, rim_ref, low, high, state_ref, edge_ref, whole_ref):
    low_ref, side_low_ref = low
    high_ref, side_high_ref = high
    last = whole_ref is not None
    row = sublanes()

    def one_band(band, carry):
        for layer in range(LAYERS):
            outside = []
            for v in range(25):
                terms = [weights[layer + 4 - i] * low_ref[band, i, v] for i in range(layer, 4)]
                terms += [weights[5 + i - layer] * high_ref[band, i, v] for i in range(layer)]
                outside.append((terms[0] + terms[1]) + (terms[2] + terms[3]))
            tiles = []
            for tile in range(3):
                cells = []
                for j in range(10):
                    if tile < 2:
                        extra = outside[tile * 10 + j]
                    elif j < 5:
                        extra = outside[20 + j]
                    else:
                        extra = pltpu.roll(outside[15 + j], 64, 1)
                    cell = part_ref[band, layer, tile, j] + extra
                    at = layer * 2 + tile if tile < 2 else 10 + layer
                    if j < 4:
                        cell += jnp.where(row == 0, rim_ref[band, 0, j, at : at + 1, :], 0.0)
                    if j >= 6:
                        cell += jnp.where(row == 7, rim_ref[band, 1, j - 6, at : at + 1, :], 0.0)
                    cells.append(cell)
                tiles.append(cells)
            if last:
                packed = tiles[0] + tiles[1] + [pair(tiles[2][j], tiles[2][j + 5]) for j in range(5)]
                for v in range(25):
                    place = layer * 25 + v
                    whole_ref[place // 32, band, place % 32] = packed[v]
            else:
                for tile in range(3):
                    for j in range(10):
                        state_ref[band, layer, tile, j] = tiles[tile][j]
                send_sides(tiles, band, layer, side_low_ref, side_high_ref)
                send_edges(tiles, band, layer, edge_ref)
        if last:
            for place in range(125, 128):
                whole_ref[place // 32, band, place % 32] = jnp.zeros((8, 128), F32)
        return carry

    lax.fori_loop(0, BANDS, one_band, 0)


def deal(whole_ref, piece_refs):
    for step, piece_ref in enumerate(piece_refs):
        piece_ref[...] = whole_ref[lax.axis_index("band") ^ step]


def collect(piece_refs, whole_ref):
    for step, piece_ref in enumerate(piece_refs):
        whole_ref[lax.axis_index("band") ^ step] = piece_ref[...]


PAIRS = [(a, b) for a in range(GROUPS * BANDS) for b in range(a + 1)]


def overlap_kernel(*refs):
    *piece_refs, whole_ref, sums_ref, row_ref = refs
    collect(piece_refs, whole_ref)

    def accumulate(quad, totals):
        for part in range(4):
            cells = [whole_ref[a // BANDS, a % BANDS, quad * 4 + part] for a in range(GROUPS * BANDS)]
            totals = tuple(total + cells[a] * cells[b] for total, (a, b) in zip(totals, PAIRS))
        return totals

    totals = lax.fori_loop(0, 8, accumulate, tuple(jnp.zeros((8, 128), F32) for _ in PAIRS))
    row_ref[...] = jnp.zeros_like(row_ref)
    for at, total in enumerate(totals):
        row_ref[at : at + 1, :] = jnp.sum(total, axis=0, keepdims=True)
    sums = lax.dot_general(
        jnp.ones((8, 128), F32),
        row_ref[...],
        (((1,), (1,)), ((), ())),
        precision=lax.Precision.HIGHEST,
        preferred_element_type=F32,
    )
    sums_ref[...] = jnp.broadcast_to(sums[0:1].reshape(1, 1, 128), sums_ref.shape)


def rotate_kernel(cell_count, whole_ref, sums_ref, *refs):
    *piece_refs, turned_ref = refs
    count = sums_ref.shape[0] // 8
    parts = [jnp.sum(sums_ref[i * count : (i + 1) * count], axis=0) for i in range(8)]
    while len(parts) > 1:
        parts = [parts[i] + parts[i + 1] for i in range(0, len(parts), 2)]
    row = parts[0] * (1.0 / cell_count)
    extent = GROUPS * BANDS
    matrix = {}
    for at, place in enumerate(PAIRS):
        matrix[place] = jnp.broadcast_to(row[:, at : at + 1], (8, 128))
    factor = {}
    scale = []
    for b in range(extent):
        running = matrix[b, b]
        for s in range(b):
            running = running - factor[b, s] * factor[b, s]
        guess = lax.rsqrt(running)
        scale.append(guess * (1.5 - (0.5 * running * guess) * guess))
        for a in range(b + 1, extent):
            running = matrix[a, b]
            for s in range(b):
                running = running - factor[a, s] * factor[b, s]
            factor[a, b] = running * scale[b]
    inverse = {}
    for target in range(extent):
        inverse[target, target] = scale[target]
        for a in range(target):
            running = factor[target, a] * inverse[a, a]
            for source in range(a + 1, target):
                running = running + factor[target, source] * inverse[source, a]
            inverse[target, a] = -running * scale[target]

    def turn(quad, carry):
        for part in range(4):
            at = quad * 4 + part
            cells = [whole_ref[a // BANDS, a % BANDS, at] for a in range(extent)]
            for j in range(extent):
                total = inverse[j, 0] * cells[0]
                for a in range(1, j + 1):
                    total = total + inverse[j, a] * cells[a]
                turned_ref[j // BANDS, j % BANDS, at] = total
        return carry

    lax.fori_loop(0, 8, turn, 0)
    deal(turned_ref, piece_refs)


def merge_kernel(*refs):
    *piece_refs, out_ref, whole_ref, stage_ref, plane_ref, sems = refs
    collect(piece_refs, whole_ref)

    def copy_out(at):
        return pltpu.make_async_copy(plane_ref.at[at], out_ref.at[at // LAYERS, at % LAYERS], sems.at[at])

    for at in range(BANDS * LAYERS):
        band, layer = at // LAYERS, at % LAYERS
        for v in range(25):
            place = layer * 25 + v
            cell = whole_ref[place // 32, band, place % 32]
            if v < 20:
                stage_ref[at, v // 10, pl.ds(v % 10, 8, stride=10), :] = cell
            else:
                stage_ref[at, 2, pl.ds(v - 20, 8, stride=10), :] = cell
                stage_ref[at, 2, pl.ds(v - 15, 8, stride=10), :] = pltpu.roll(cell, 64, 1)
        for tile in range(2):
            plane_ref[at, :, tile * 128 : tile * 128 + 128] = stage_ref[at, tile]
        plane_ref[at, :, 256:320] = stage_ref[at, 2, :, 0:64]
        copy_out(at).start()
    for at in range(BANDS * LAYERS):
        copy_out(at).wait()


def swapped(array, axis, partner):
    return lax.ppermute(array, axis, [(i, partner(i)) for i in range(lax.axis_size(axis))])


def beside(array, axis, offset):
    count = lax.axis_size(axis)
    return swapped(array, axis, lambda i: (i + (offset if i % 2 == 0 else -offset)) % count)


def exchange(pieces):
    moved = {step: swapped(pieces[step], "band", lambda i: i ^ step) for step in (2, 1, 3)}
    return [pieces[0], moved[1], moved[2], moved[3]]


def local(band_fields, potential, cutoff, upper_bound):
    devices = lax.axis_size("dx") * lax.axis_size("dy") * lax.axis_size("band")
    cell_count = float(LAYERS * 80 * 320 * lax.axis_size("dx") * lax.axis_size("dy"))
    cutoff = cutoff.reshape(1, 1)
    upper_bound = upper_bound.reshape(1, 1)
    stage = (3, 80, 128)
    edges = (2, BANDS, 56, 128)
    state, far, near, inner, outer = call(
        split_kernel, (STATE, SIDE, SIDE, EDGE, EDGE), scratch=(stage, edges)
    )(band_fields)
    previous = diagonal = None
    for step in range(4):
        first, last = step == 0, step == 3
        far = beside(far, "dx", -1)
        near = beside(near, "dx", 1)
        inner = beside(inner, "dy", 1)
        outer = beside(outer, "dy", -1)
        wide = (3, 10, 8, 128)
        if first:
            part, diagonal = call(
                functools.partial(inner_kernel, True), (STATE, STATE[1:]), scratch=(wide, stage)
            )(state, potential, cutoff, upper_bound)
        else:
            (part,) = call(functools.partial(inner_kernel, False), (STATE,), scratch=(wide,))(
                state, previous, diagonal, cutoff, upper_bound
            )
        previous = state
        arguments = (part, far, near, inner, outer, cutoff, upper_bound)
        rim = (BANDS, 2, 4, 24, 128)
        if last:
            pieces = call(
                functools.partial(outer_kernel, first, last),
                (PIECE,) * 4,
                scratch=(rim, (GROUPS,) + PIECE),
            )(*arguments)
        else:
            state, far, near, inner, outer = call(
                functools.partial(outer_kernel, first, last),
                (STATE, SIDE, SIDE, EDGE, EDGE),
                scratch=(rim, edges),
            )(*arguments)
    pieces = exchange(pieces)
    whole, sums = call(overlap_kernel, ((GROUPS,) + PIECE, (devices, 1, 128)), scratch=((128, 128),))(*pieces)
    sums = lax.all_to_all(sums, ("dy", "band", "dx"), 0, 0)
    pieces = call(
        functools.partial(rotate_kernel, cell_count), (PIECE,) * 4, scratch=((GROUPS,) + PIECE,)
    )(whole, sums)
    pieces = exchange(pieces)
    planes = BANDS * LAYERS
    (rotated,) = call(
        merge_kernel,
        ((BANDS, LAYERS, 80, 320),),
        scratch=((GROUPS,) + PIECE, (planes,) + stage, (planes, 80, 320)),
        semaphores=planes,
        out_specs=(pl.BlockSpec(memory_space=pl.ANY),),
    )(*pieces)
    return rotated


def solution(mesh):
    in_specs = (P("band", "dx", "dy", None), P("dx", "dy", None), P(), P())
    out_specs = P("band", "dx", "dy", None)
    return jax.shard_map(local, mesh=mesh, in_specs=in_specs, out_specs=out_specs, check_vma=False)
```
